128 devices in a mesh: enc: 4 (over x), dp: 32 (over z, y, core).
Axes of the slice: x: 4, y: 4, z: 4, core: 2. Of those that a mesh axis runs over, the one named last changes fastest.
Arguments:
- queries: bfloat16 [512, 64, 2048], P('dp', None, 'enc'), may hold values from -6 to 6
- encodings: bfloat16 [2048, 128, 512], P(('enc', 'dp')), may hold values from -6 to 6
- w_key: bfloat16 [512, 2048], P(None, 'enc'), may hold values from -0.25 to 0.25
- w_value: bfloat16 [512, 2048], P(None, 'enc'), may hold values from -0.25 to 0.25
- neighbours: int32 [512, 2], P('dp'), may hold values from 0 to 2047, as said below
- d_out: bfloat16 [512, 64, 2048], P('dp', None, 'enc'), may hold values from -48 to 48
Outputs:
- attended: bfloat16 [512, 64, 2048], P('dp', None, 'enc')
- d_queries: bfloat16 [512, 64, 2048], P('dp', None, 'enc')
- d_encodings: bfloat16 [2048, 128, 512], P(('enc', 'dp'))
- d_w_key: float32 [512, 2048], P('dp', 'enc')
- d_w_value: float32 [512, 2048], P('dp', 'enc')
The draws below stay inside these ranges and needn't reach their ends.
Inputs may be any that keep to these rules, and one draw needn't show every extreme that they name: Neighbour n is held by the device at flat index n // 16 of enc+dp. No neighbour is named twice among the stretches of one dp index. The stretches of one dp index name at most 2 neighbours held by one device, and some device is named exactly 2 times by the stretches of every dp index. Of the 32 pairs of one dp index at most 12 name neighbours of one encoder group, and exactly that many do in some group.
All inputs are finite; a program needn't handle non-finite values.
Results may differ from the reference program's by a relative error of at most 0.025.
Values may be sent and summed in bfloat16 or wider, within the bound.
No kernel may reach another device: no remote copies, remote signals or barrier semaphores. Data moves between devices by JAX's collectives and lax.ppermute only.
A program may use at most 256 MiB of HBM per device.

```python
import math
import jax
import jax.numpy as jnp
from jax import lax

HEADS = 16
D_HEAD = 128
ENC = 512
STRETCH = 64
NLEN = 128
KNB = 2
CH_DEV = 16
NB_DEV = 16
CAP = 2
HD = 2048
PAIR_G = 12
STRETCHES = 512
NEIGH = 2048
N_ENC = 4
N_DP = 32


def draw_neighbours(key, part):
    key = jax.random.fold_in(key, 11)
    pair_count = KNB * CH_DEV
    remaining = pair_count - PAIR_G
    slot_total = CAP * N_DP
    hot_key = jax.random.fold_in(key, 1)
    hot_group = jax.random.randint(hot_key, (), 0, N_ENC)
    hot_shard = jax.random.randint(jax.random.fold_in(hot_key, 2), (), 0, N_DP)
    slot_ids = jnp.arange(slot_total, dtype=jnp.int32)
    group_ids = jnp.arange(N_ENC, dtype=jnp.int32)

    def group_slots(group_key, group_id):
        rank_order = jax.random.permutation(group_key, slot_total).astype(jnp.int32)
        forced = jnp.logical_and(group_id == hot_group, slot_ids // CAP == hot_shard)
        rank_order = rank_order + slot_total * (1 - forced.astype(jnp.int32))
        return jnp.argsort(rank_order, stable=True).astype(jnp.int32)

    def one_shard(shard_key):
        sub_keys = jax.random.split(shard_key, 6)
        busy_group = jax.random.randint(sub_keys[0], (), 0, N_ENC)
        first_share = jax.random.randint(sub_keys[1], (), remaining // 4, remaining * 3 // 8)
        second_share = jax.random.randint(sub_keys[2], (), remaining // 4, remaining * 3 // 8)
        others = jnp.stack([first_share, second_share, remaining - first_share - second_share])
        position = jnp.clip(group_ids - (group_ids > busy_group).astype(jnp.int32), 0, N_ENC - 2)
        counts = jnp.where(group_ids == busy_group, PAIR_G, others[position])
        chosen = jax.vmap(group_slots)(jax.random.split(sub_keys[3], N_ENC), group_ids)
        is_valid = slot_ids[None, :] < counts[:, None]
        owner_flat = group_ids[:, None] * N_DP + chosen // CAP
        row_pick = jax.random.randint(sub_keys[4], (N_ENC, slot_total), 0, NB_DEV // CAP) * CAP + chosen % CAP
        neighbour_ids = (owner_flat * NB_DEV + row_pick).reshape(-1)
        keep_order = jnp.argsort((1 - is_valid.astype(jnp.int32)).reshape(-1), stable=True)[:pair_count]
        selected = neighbour_ids[keep_order]
        shuffled = selected[jax.random.permutation(sub_keys[5], pair_count)]
        return shuffled.reshape(CH_DEV, KNB).astype(jnp.int32)
    shard_keys = jax.random.split(jax.random.fold_in(key, 3), N_DP)
    return jax.vmap(one_shard)(shard_keys).reshape(CH_DEV * N_DP, KNB)


def level_of(rng, shape, cuts, low, high):
    factor_of, own = 1.0, jax.random.fold_in(rng, 6)
    for axis_at, parts in cuts:
        draws = jnp.exp(jax.random.uniform(jax.random.fold_in(own, axis_at), (parts,), jnp.float32, low / len(cuts), high / len(cuts)))
        factor_of = factor_of * jnp.repeat(draws, shape[axis_at] // parts).reshape([-1 if axis == axis_at else 1 for axis in range(len(shape))])
    return factor_of


def bell_draw(own_key, dims, spread, limit, cuts=(), held_as=jnp.bfloat16):
    array = jax.random.normal(own_key, dims, jnp.float32) * spread
    if len(cuts) > 0:
        array = level_of(own_key, dims, cuts, -0.22, 0.18) * array
    return jnp.clip(array, min=-limit, max=limit).astype(held_as)


def setup_inputs(seed: int = 0) -> dict:
    streams_of = jax.random.split(jax.random.key(seed), 7)
    return {
        "queries": bell_draw(streams_of[0], (STRETCHES, STRETCH, HD), 1.0, 6.0, ((0, 32), (2, 4))),
        "encodings": bell_draw(streams_of[1], (NEIGH, NLEN, ENC), 1.0, 6.0, ((0, 128),)),
        "w_key": bell_draw(streams_of[2], (ENC, HD), ENC ** -0.5, 0.25, ((1, 4),)),
        "w_value": bell_draw(streams_of[3], (ENC, HD), ENC ** -0.5, 0.25, ((1, 4),)),
        "neighbours": draw_neighbours(jax.random.fold_in(streams_of[6], 71), 0),
        "d_out": bell_draw(streams_of[5], (STRETCHES, STRETCH, HD), 8.0, 48.0, ((0, 32), (2, 4))),
    }


EPSILON = 1e-06

def rounded(values):
    return lax.optimization_barrier(values.astype(jnp.bfloat16))

def unit_rows(values):
    factor = lax.rsqrt(lax.optimization_barrier(jnp.mean(values * values, axis=-1, keepdims=True)) + EPSILON)
    return (values * factor, factor)

def unit_grad(gradient, unit_vals, factor):
    return factor * (gradient - unit_vals * lax.optimization_barrier(jnp.mean(gradient * unit_vals, axis=-1, keepdims=True)))

def reference(queries, encodings, w_key, w_value, neighbours, d_out):
    inverse = 1.0 / math.sqrt(D_HEAD)
    pair_count = KNB * CH_DEV
    group_cols = HD // N_ENC
    query_blocks = queries.reshape(N_DP, CH_DEV, STRETCH, HEADS, D_HEAD)
    grad_blocks = d_out.reshape(N_DP, CH_DEV, STRETCH, HEADS, D_HEAD)
    id_blocks = neighbours.reshape(N_DP, pair_count).astype(jnp.int32)
    contract = (((0,), (0,)), ((), ()))

    def advance(totals, shard_block):
        enc_grad, key_grad, value_grad = totals
        query_block, grad_out, pair_ids = shard_block
        pair_rows = jnp.take(encodings, pair_ids, axis=0).reshape(pair_count * NLEN, ENC)
        key_rows = jnp.dot(pair_rows, w_key, preferred_element_type=jnp.float32).astype(jnp.bfloat16)
        value_rows = jnp.dot(pair_rows, w_value, preferred_element_type=jnp.float32).astype(jnp.bfloat16)
        key_heads = key_rows.reshape(CH_DEV, KNB * NLEN, HEADS, D_HEAD)
        value_heads = lax.optimization_barrier(value_rows).astype(jnp.float32).reshape(CH_DEV, KNB * NLEN, HEADS, D_HEAD)
        query_unit, query_scale = unit_rows(query_block.astype(jnp.float32))
        key_unit, key_scale = unit_rows(lax.optimization_barrier(key_heads).astype(jnp.float32))
        query_bf = rounded(query_unit).astype(jnp.float32)
        key_bf = rounded(key_unit).astype(jnp.float32)
        scores = jnp.einsum('cqhd,ckhd->chqk', query_bf, key_bf) * inverse
        raised = jnp.exp(scores)
        weights = raised / lax.optimization_barrier(jnp.sum(raised, axis=-1, keepdims=True))
        probabilities = rounded(weights).astype(jnp.float32)
        attended = jnp.einsum('chqk,ckhd->cqhd', probabilities, value_heads).astype(jnp.bfloat16)
        grad_heads = grad_out.astype(jnp.float32)
        d_probs = jnp.einsum('cqhd,ckhd->chqk', grad_heads, value_heads)
        d_scores = rounded(weights * (d_probs - lax.optimization_barrier(jnp.sum(d_probs * weights, axis=-1, keepdims=True))) * inverse).astype(jnp.float32)
        d_query_unit = jnp.einsum('chqk,ckhd->cqhd', d_scores, key_bf)
        d_queries = unit_grad(d_query_unit, query_unit, query_scale).astype(jnp.bfloat16)
        d_key_unit = jnp.einsum('chqk,cqhd->ckhd', d_scores, query_bf)
        d_keys = rounded(unit_grad(d_key_unit, key_unit, key_scale)).reshape(pair_count * NLEN, HD)
        d_values = rounded(jnp.einsum('chqk,cqhd->ckhd', probabilities, grad_heads)).reshape(pair_count * NLEN, HD)
        summed = jnp.zeros((pair_count * NLEN, ENC), jnp.float32)
        for head_group in range(N_ENC):
            low_col = head_group * group_cols
            high_col = low_col + group_cols
            partial_value = jnp.dot(d_keys[:, low_col:high_col], w_key[:, low_col:high_col].T, preferred_element_type=jnp.float32)
            partial_value = partial_value + jnp.dot(d_values[:, low_col:high_col], w_value[:, low_col:high_col].T, preferred_element_type=jnp.float32)
            summed = summed + rounded(partial_value).astype(jnp.float32)
        pair_terms = rounded(summed).astype(jnp.float32).reshape(pair_count, NLEN, ENC)
        enc_grad = enc_grad.at[pair_ids].add(pair_terms)
        key_grad = key_grad + lax.dot_general(pair_rows, d_keys, contract, preferred_element_type=jnp.float32)
        value_grad = value_grad + lax.dot_general(pair_rows, d_values, contract, preferred_element_type=jnp.float32)
        return ((enc_grad, key_grad, value_grad), (attended.reshape(CH_DEV, STRETCH, HD), d_queries.reshape(CH_DEV, STRETCH, HD)))
    start = (jnp.zeros((NEIGH, NLEN, ENC), jnp.float32), jnp.zeros((ENC, HD), jnp.float32), jnp.zeros((ENC, HD), jnp.float32))
    finals, outputs = lax.scan(advance, start, (query_blocks, grad_blocks, id_blocks))
    enc_grad, key_grad, value_grad = finals
    attended, d_queries = outputs
    return (attended.reshape(STRETCHES, STRETCH, HD), d_queries.reshape(STRETCHES, STRETCH, HD), enc_grad.astype(jnp.bfloat16), key_grad, value_grad)
```

```python
import functools
import math

import jax
import jax.numpy as jnp
from jax import lax
from jax.experimental import pallas as pl
from jax.experimental.pallas import tpu as pltpu
from jax.sharding import PartitionSpec as P

D_HEAD = 128
EPSILON = 1e-06
BOTH = ("enc", "dp")
CHUNKS = 1
PER_STEP = 1
F32 = jnp.float32
BF16 = jnp.bfloat16
ROWS = (((0,), (0,)), ((), ()))
COLS = (((1,), (1,)), ((), ()))


def mm(a, b, dims=(((1,), (0,)), ((), ()))):
    return lax.dot_general(a, b, dims, preferred_element_type=F32)


def attention_kernel(first, x_ref, q_ref, do_ref, w_ref, wt_ref, *refs):
    if first:
        att_ref, dq_ref, part_ref, dw_ref, acc = refs
    else:
        acc_in, _, _, att_ref, dq_ref, part_ref, dw_ref, acc = refs
    step = pl.program_id(0)
    inverse = 1.0 / math.sqrt(D_HEAD)
    per_step, span, cols = q_ref.shape
    sources, pairs, rows, width = x_ref.shape
    knb = pairs // per_step
    keys_n = sources * knb * rows
    heads = cols // D_HEAD

    @pl.when(step == 0)
    def _():
        acc[...] = jnp.zeros_like(acc) if first else acc_in[...]

    for s in range(per_step):
        x = x_ref[:, s * knb : (s + 1) * knb].reshape(keys_n, width)
        kv = mm(x, w_ref[...]).astype(BF16)
        d_key_parts, d_value_parts = [], []
        for h in range(heads):
            at = slice(h * D_HEAD, (h + 1) * D_HEAD)
            query = q_ref[s, :, at].astype(F32)
            grad = do_ref[s, :, at]
            key = kv[:, at].astype(F32)
            value = kv[:, cols + h * D_HEAD : cols + (h + 1) * D_HEAD]
            query_scale = lax.rsqrt(jnp.mean(query * query, axis=-1, keepdims=True) + EPSILON)
            query_unit = query * query_scale
            query_bf = query_unit.astype(BF16)
            key_scale = lax.rsqrt(jnp.mean(key * key, axis=-1, keepdims=True) + EPSILON)
            key_unit = key * key_scale
            key_bf = key_unit.astype(BF16)
            raised = jnp.exp(mm(query_bf, key_bf, COLS) * inverse)
            weights = raised * (1.0 / jnp.sum(raised, axis=-1, keepdims=True))
            probs = weights.astype(BF16)
            att_ref[s, :, at] = mm(probs, value).astype(BF16)
            d_probs = mm(grad, value, COLS)
            inner = jnp.sum(d_probs * weights, axis=-1, keepdims=True)
            d_scores = (weights * (d_probs - inner) * inverse).astype(BF16)
            d_query_unit = mm(d_scores, key_bf)
            mean_q = jnp.mean(d_query_unit * query_unit, axis=-1, keepdims=True)
            dq_ref[s, :, at] = (query_scale * (d_query_unit - query_unit * mean_q)).astype(BF16)
            d_key_unit = mm(d_scores, query_bf, ROWS)
            mean_k = jnp.mean(d_key_unit * key_unit, axis=-1, keepdims=True)
            d_key_parts.append((key_scale * (d_key_unit - key_unit * mean_k)).astype(BF16))
            d_value_parts.append(mm(probs, grad, ROWS).astype(BF16))
        d_kv = jnp.concatenate(d_key_parts + d_value_parts, axis=1)
        part = mm(d_kv, wt_ref[...]).astype(BF16)
        part_ref[:, s * knb : (s + 1) * knb] = part.reshape(sources, knb, rows, width)
        acc[...] += mm(x, d_kv, ROWS)

    @pl.when(step == pl.num_programs(0) - 1)
    def _():
        dw_ref[...] = acc[...].astype(dw_ref.dtype)


def attention(chunk, chunks, x, queries, d_out, w, wt, carried):
    stretches, span, cols = queries.shape
    sources, pairs, rows, width = x.shape
    mine = stretches // chunks
    knb = pairs // mine
    steps = mine // PER_STEP
    first, last = chunk == 0, chunk == chunks - 1
    offset = chunk * steps
    by_stretch = pl.BlockSpec((PER_STEP, span, cols), lambda i: (offset + i, 0, 0))
    by_pair = pl.BlockSpec((sources, PER_STEP * knb, rows, width), lambda i: (0, i, 0, 0))
    whole = lambda shape: pl.BlockSpec(shape, lambda i: (0,) * len(shape))
    in_specs = [by_pair, by_stretch, by_stretch, whole(w.shape), whole(wt.shape)]
    args = [x, queries, d_out, w, wt]
    aliases = {}
    if not first:
        att, dq, acc = carried
        in_specs += [whole(acc.shape), pl.BlockSpec(memory_space=pl.ANY), pl.BlockSpec(memory_space=pl.ANY)]
        args += [acc, att, dq]
        aliases = {6: 0, 7: 1}
    return pl.pallas_call(
        functools.partial(attention_kernel, first),
        grid=(steps,),
        in_specs=in_specs,
        out_specs=[by_stretch, by_stretch, by_pair, whole(w.shape)],
        out_shape=[
            jax.ShapeDtypeStruct(queries.shape, BF16),
            jax.ShapeDtypeStruct(queries.shape, BF16),
            jax.ShapeDtypeStruct(x.shape, BF16),
            jax.ShapeDtypeStruct(w.shape, BF16 if last else F32),
        ],
        scratch_shapes=[pltpu.VMEM(w.shape, F32)],
        input_output_aliases=aliases,
        compiler_params=pltpu.CompilerParams(vmem_limit_bytes=48 * 1024 * 1024),
        cost_estimate=pl.CostEstimate(
            flops=mine * 900_000_000, bytes_accessed=mine * 800_000, transcendentals=mine * 66_000
        ),
        name="attention",
    )(*args)


def pick_kernel(ids_ref, table_ref, out_ref):
    ids = ids_ref[...]
    count = table_ref.shape[0]
    hit = ids == lax.broadcasted_iota(jnp.int32, (ids.shape[0], count), 1)
    out_ref[...] = mm(hit.astype(BF16), table_ref[...]).astype(BF16)


def pick_rows(ids, table, tile=256):
    count, width = table.shape
    wanted = ids.shape[0]
    return pl.pallas_call(
        pick_kernel,
        grid=(wanted // tile,),
        in_specs=[
            pl.BlockSpec((tile, 1), lambda i: (i, 0)),
            pl.BlockSpec((count, width), lambda i: (0, 0)),
        ],
        out_specs=pl.BlockSpec((tile, width), lambda i: (i, 0)),
        out_shape=jax.ShapeDtypeStruct((wanted, width), BF16),
        compiler_params=pltpu.CompilerParams(vmem_limit_bytes=48 * 1024 * 1024),
        name="pick_rows",
    )(ids.reshape(wanted, 1), table)


def place_kernel(ids_ref, rows_ref, out_ref):
    ids = ids_ref[...]
    tile = out_ref.shape[0]
    row = lax.broadcasted_iota(jnp.int32, (tile, ids.shape[1]), 0) + pl.program_id(0) * tile
    out_ref[...] = mm((ids == row).astype(BF16), rows_ref[...]).astype(BF16)


def place_rows(ids, rows, count, tile=256):
    given, width = rows.shape
    return pl.pallas_call(
        place_kernel,
        grid=(count // tile,),
        in_specs=[
            pl.BlockSpec((1, given), lambda i: (0, 0)),
            pl.BlockSpec((given, width), lambda i: (0, 0)),
        ],
        out_specs=pl.BlockSpec((tile, width), lambda i: (i, 0)),
        out_shape=jax.ShapeDtypeStruct((count, width), BF16),
        compiler_params=pltpu.CompilerParams(vmem_limit_bytes=48 * 1024 * 1024),
        name="place_rows",
    )(ids.reshape(1, given), rows)


def body(queries, encodings, w_key, w_value, neighbours, d_out):
    enc_count = lax.axis_size("enc")
    shards = lax.axis_size("dp")
    devices = enc_count * shards
    held, neigh_len, width = encodings.shape
    stretches, _, cols = queries.shape
    pair_count = neighbours.size
    per_chunk = pair_count // CHUNKS
    w = jnp.concatenate([w_key, w_value], axis=1)
    wt = w.T
    ids = lax.all_gather(neighbours.reshape(-1), "dp", axis=0, tiled=True)
    ids = ids.reshape(shards, CHUNKS, per_chunk)
    by_row = jnp.swapaxes(encodings, 0, 1)
    table = lax.all_to_all(by_row, BOTH, 0, 0, tiled=True).reshape(devices * held, width)
    inputs = []
    for c in range(CHUNKS):
        sent = pick_rows(ids[:, c].reshape(-1), table).reshape(shards, per_chunk, width)
        got = lax.all_to_all(sent, "dp", 0, 0, tiled=True)
        inputs.append(lax.all_gather(jnp.swapaxes(got, 0, 1), "enc", axis=0, tiled=False))
    carried = None
    returned = []
    for c in range(CHUNKS):
        att, dq, part, acc = attention(c, CHUNKS, inputs[c], queries, d_out, w, wt, carried)
        carried = (att, dq, acc)
        summed = lax.psum_scatter(part, "enc", scatter_dimension=0, tiled=False)
        back = lax.all_to_all(jnp.swapaxes(summed, 0, 1), "dp", 0, 0, tiled=True)
        returned.append(back.reshape(shards * per_chunk, width))
    order = jnp.swapaxes(ids, 0, 1).reshape(-1)
    rows = jnp.concatenate(returned, axis=0) if CHUNKS > 1 else returned[0]
    placed = place_rows(order, rows, devices * held).reshape(devices, held, width)
    d_encodings = jnp.swapaxes(lax.all_to_all(placed, BOTH, 0, 0, tiled=True), 0, 1)
    d_w = lax.all_to_all(acc.reshape(shards, -1, 2 * cols), "dp", 0, 0, tiled=True)
    d_w = jnp.sum(d_w.astype(F32), axis=0)
    return att, dq, d_encodings, d_w[:, :cols], d_w[:, cols:]


def solution(mesh):
    in_specs = (
        P("dp", None, "enc"),
        P(("enc", "dp"), None, None),
        P(None, "enc"),
        P(None, "enc"),
        P("dp", None),
        P("dp", None, "enc"),
    )
    out_specs = (
        P("dp", None, "enc"),
        P("dp", None, "enc"),
        P(("enc", "dp"), None, None),
        P("dp", "enc"),
        P("dp", "enc"),
    )
    return jax.shard_map(body, mesh=mesh, in_specs=in_specs, out_specs=out_specs, check_vma=False)
```

```python
import functools
import math

import jax
import jax.numpy as jnp
from jax import lax
from jax.experimental import pallas as pl
from jax.experimental.pallas import tpu as pltpu
from jax.sharding import PartitionSpec as P

D_HEAD = 128
EPSILON = 1e-06
BOTH = ("enc", "dp")
CHUNKS = (8, 8)
PER_STEP = 2
PIECES = 4
FAR_FIRST = (2, 1, -1)
F32 = jnp.float32
BF16 = jnp.bfloat16
ROWS = (((0,), (0,)), ((), ()))
COLS = (((1,), (1,)), ((), ()))


def mm(a, b, dims=(((1,), (0,)), ((), ()))):
    return lax.dot_general(a, b, dims, preferred_element_type=F32)


def mean(value):
    return jnp.mean(value, axis=-1, keepdims=True)


def attention_kernel(first, *refs):
    x_refs, (q_ref, do_ref, w_ref) = refs[:PIECES], refs[PIECES : PIECES + 3]
    acc_in = None if first else refs[PIECES + 3]
    att_ref, dq_ref, *part_refs, dw_ref, acc = refs[PIECES + (3 if first else 6) :]
    step = pl.program_id(0)
    inverse = 1.0 / math.sqrt(D_HEAD)
    per_step, span, cols = q_ref.shape
    pairs, rows, width = x_refs[0].shape
    knb = pairs // per_step
    heads = cols // D_HEAD

    @pl.when(step == 0)
    def _():
        acc[...] = jnp.zeros_like(acc) if first else acc_in[...]

    heads_at = [slice(h * D_HEAD, (h + 1) * D_HEAD) for h in range(heads)]
    each = lambda f, *lists: [f(*parts) for parts in zip(*lists)]
    x = jnp.concatenate(
        [ref[s * knb : (s + 1) * knb].reshape(knb * rows, width) for s in range(per_step) for ref in x_refs], axis=0
    )
    count = knb * rows * len(x_refs)
    spans = [slice(s * count, (s + 1) * count) for s in range(per_step)]
    both = [(s, at) for s in range(per_step) for at in heads_at]
    queries = [q_ref[s, :, at].astype(F32) for s, at in both]
    grads = [do_ref[s, :, at] for s, at in both]
    query_scales = each(lambda q: lax.rsqrt(mean(q * q) + EPSILON), queries)
    query_units = each(lambda q, c: q * c, queries, query_scales)
    query_bfs = each(lambda u: u.astype(BF16), query_units)
    keys_all = mm(x, w_ref[:, :cols]).astype(BF16).astype(F32)
    keys = [keys_all[spans[s], at] for s, at in both]
    key_scales = each(lambda k: lax.rsqrt(mean(k * k) + EPSILON), keys)
    key_units = each(lambda k, c: k * c, keys, key_scales)
    key_bfs = each(lambda u: u.astype(BF16), key_units)
    values_all = mm(x, w_ref[:, cols:]).astype(BF16)
    values = [values_all[spans[s], at] for s, at in both]
    raised = each(lambda q, k: jnp.exp(mm(q, k, COLS) * inverse), query_bfs, key_bfs)
    d_probs = each(lambda g, v: mm(g, v, COLS), grads, values)
    weights = each(lambda e: e * (1.0 / jnp.sum(e, axis=-1, keepdims=True)), raised)
    probs = each(lambda p: p.astype(BF16), weights)
    attended = each(lambda p, v: mm(p, v).astype(BF16), probs, values)
    d_values = each(lambda p, g: mm(p, g, ROWS).astype(BF16), probs, grads)
    d_scores = each(
        lambda p, d: (p * (d - jnp.sum(d * p, axis=-1, keepdims=True)) * inverse).astype(BF16), weights, d_probs
    )
    d_query_units = each(lambda d, k: mm(d, k), d_scores, key_bfs)
    d_key_units = each(lambda d, q: mm(d, q, ROWS), d_scores, query_bfs)
    d_queries = each(
        lambda c, d, u: (c * (d - u * mean(d * u))).astype(BF16), query_scales, d_query_units, query_units
    )
    d_keys = each(lambda c, d, u: (c * (d - u * mean(d * u))).astype(BF16), key_scales, d_key_units, key_units)
    d_kv = []
    for s in range(per_step):
        mine = slice(s * heads, (s + 1) * heads)
        att_ref[s] = jnp.concatenate(attended[mine], axis=1)
        dq_ref[s] = jnp.concatenate(d_queries[mine], axis=1)
        d_kv.append(jnp.concatenate(d_keys[mine] + d_values[mine], axis=1))
    d_kv = jnp.concatenate(d_kv, axis=0)
    part = mm(d_kv, w_ref[...], COLS).astype(BF16)
    for s in range(per_step):
        for i, ref in enumerate(part_refs):
            at = s * count + i * knb * rows
            ref[s * knb : (s + 1) * knb] = part[at : at + knb * rows].reshape(knb, rows, width)
    acc[...] += mm(x, d_kv, ROWS)

    @pl.when(step == pl.num_programs(0) - 1)
    def _():
        dw_ref[...] = acc[...].astype(dw_ref.dtype)


def attention(chunk, pieces, queries, d_out, w, carried):
    _, span, cols = queries.shape
    pairs, rows, width = pieces[0].shape
    mine = CHUNKS[chunk]
    knb = pairs // mine
    steps = mine // PER_STEP
    first, last = chunk == 0, chunk == len(CHUNKS) - 1
    offset = sum(CHUNKS[:chunk]) // PER_STEP
    by_stretch = pl.BlockSpec((PER_STEP, span, cols), lambda i: (offset + i, 0, 0))
    by_pair = pl.BlockSpec((PER_STEP * knb, rows, width), lambda i: (i, 0, 0))
    whole = pl.BlockSpec(w.shape, lambda i: (0, 0))
    in_specs = [by_pair] * PIECES + [by_stretch] * 2 + [whole]
    args = [*pieces, queries, d_out, w]
    aliases = {}
    if not first:
        att, dq, acc = carried
        in_specs += [whole, pl.BlockSpec(memory_space=pl.ANY), pl.BlockSpec(memory_space=pl.ANY)]
        args += [acc, att, dq]
        aliases = {PIECES + 4: 0, PIECES + 5: 1}
    out = pl.pallas_call(
        functools.partial(attention_kernel, first),
        grid=(steps,),
        in_specs=in_specs,
        out_specs=[by_stretch, by_stretch] + [by_pair] * PIECES + [whole],
        out_shape=[jax.ShapeDtypeStruct(queries.shape, BF16)] * 2
        + [jax.ShapeDtypeStruct((pairs, rows, width), BF16)] * PIECES
        + [jax.ShapeDtypeStruct(w.shape, BF16 if last else F32)],
        scratch_shapes=[pltpu.VMEM(w.shape, F32)],
        input_output_aliases=aliases,
        compiler_params=pltpu.CompilerParams(vmem_limit_bytes=40 * 1024 * 1024),
        cost_estimate=pl.CostEstimate(
            flops=mine * 900_000_000, bytes_accessed=mine * 800_000, transcendentals=mine * 66_000
        ),
        name="attention",
    )(*args)
    return out[2:-1], (out[0], out[1], out[-1])


def pick_kernel(ids_ref, table_ref, out_ref):
    ids = ids_ref[...]
    count = table_ref.shape[0]
    hit = ids == lax.broadcasted_iota(jnp.int32, (ids.shape[0], count), 1)
    out_ref[...] = mm(hit.astype(BF16), table_ref[...]).astype(BF16)


def pick_rows(ids, table, tile=256):
    count, width = table.shape
    wanted = ids.shape[0]
    return pl.pallas_call(
        pick_kernel,
        grid=(wanted // tile,),
        in_specs=[
            pl.BlockSpec((tile, 1), lambda i: (i, 0)),
            pl.BlockSpec((count, width), lambda i: (0, 0)),
        ],
        out_specs=pl.BlockSpec((tile, width), lambda i: (i, 0)),
        out_shape=jax.ShapeDtypeStruct((wanted, width), BF16),
        compiler_params=pltpu.CompilerParams(vmem_limit_bytes=48 * 1024 * 1024),
        name="pick_rows",
    )(ids.reshape(wanted, 1), table)


def place_kernel(ids_ref, rows_ref, out_ref):
    ids = ids_ref[...]
    tile = out_ref.shape[0]
    row = lax.broadcasted_iota(jnp.int32, (tile, ids.shape[1]), 0) + pl.program_id(0) * tile
    out_ref[...] = mm((ids == row).astype(BF16), rows_ref[...]).astype(BF16)


def place_rows(ids, rows, count, tile=256):
    given, width = rows.shape
    return pl.pallas_call(
        place_kernel,
        grid=(count // tile,),
        in_specs=[
            pl.BlockSpec((1, given), lambda i: (0, 0)),
            pl.BlockSpec((given, width), lambda i: (0, 0)),
        ],
        out_specs=pl.BlockSpec((tile, width), lambda i: (i, 0)),
        out_shape=jax.ShapeDtypeStruct((count, width), BF16),
        compiler_params=pltpu.CompilerParams(vmem_limit_bytes=48 * 1024 * 1024),
        name="place_rows",
    )(ids.reshape(1, given), rows)


def shift(value, by):
    count = lax.axis_size("enc")
    return lax.ppermute(value, "enc", [(i, (i + by) % count) for i in range(count)])


def gather_pieces(own):
    return [own] + [shift(own, by) for by in FAR_FIRST]


def sum_pieces(parts):
    back = [shift(part, -by) for by, part in zip(FAR_FIRST, parts[1:])]
    return sum(part.astype(F32) for part in [parts[0], *back]).astype(BF16)


def body(queries, encodings, w_key, w_value, neighbours, d_out):
    enc_count = lax.axis_size("enc")
    shards = lax.axis_size("dp")
    devices = enc_count * shards
    held, neigh_len, width = encodings.shape
    stretches, _, cols = queries.shape
    pair_count = neighbours.size
    w = jnp.concatenate([w_key, w_value], axis=1)
    own_ids = jnp.broadcast_to(neighbours.reshape(1, -1), (shards, pair_count))
    ids = lax.all_to_all(own_ids, "dp", 0, 0, tiled=True).reshape(-1)
    by_row = jnp.swapaxes(encodings, 0, 1)
    table = lax.all_to_all(by_row, BOTH, 0, 0, tiled=True).reshape(devices * held, width)
    knb = pair_count // stretches
    sent, start = [], 0
    for size in CHUNKS:
        wanted = ids.reshape(shards, pair_count)[:, start * knb : (start + size) * knb]
        sent.append(pick_rows(wanted.reshape(-1), table).reshape(shards, size * knb, width))
        start += size
    pieces = []
    for c in range(len(CHUNKS)):
        if c > 0:
            sent[c], own = lax.optimization_barrier((sent[c], own))
            pieces.append(gather_pieces(own))
        own = jnp.swapaxes(lax.all_to_all(sent[c], "dp", 0, 0, tiled=True), 0, 1)
    pieces.append(gather_pieces(own))
    carried = None
    returned = []
    for c in range(len(CHUNKS)):
        parts, carried = attention(c, pieces[c], queries, d_out, w, carried)
        returned.append(sum_pieces(parts))
    att, dq, acc = carried
    d_w = lax.all_to_all(acc.reshape(shards, -1, 2 * cols), "dp", 0, 0, tiled=True)
    summed = jnp.swapaxes(jnp.concatenate(returned, axis=0), 0, 1)
    summed, d_w = lax.optimization_barrier((summed, d_w))
    rows = lax.all_to_all(summed, "dp", 0, 0, tiled=True).reshape(shards * pair_count, width)
    placed = place_rows(ids, rows, devices * held).reshape(devices, held, width)
    d_encodings = jnp.swapaxes(lax.all_to_all(placed, BOTH, 0, 0, tiled=True), 0, 1)
    d_w = jnp.sum(d_w.astype(F32), axis=0)
    return att, dq, d_encodings, d_w[:, :cols], d_w[:, cols:]


def solution(mesh):
    in_specs = (
        P("dp", None, "enc"),
        P(("enc", "dp"), None, None),
        P(None, "enc"),
        P(None, "enc"),
        P("dp", None),
        P("dp", None, "enc"),
    )
    out_specs = (
        P("dp", None, "enc"),
        P("dp", None, "enc"),
        P(("enc", "dp"), None, None),
        P("dp", "enc"),
        P("dp", "enc"),
    )
    return jax.shard_map(body, mesh=mesh, in_specs=in_specs, out_specs=out_specs, check_vma=False)
```

```python
import functools
import math

import jax
import jax.numpy as jnp
from jax import lax
from jax.experimental import pallas as pl
from jax.experimental.pallas import tpu as pltpu
from jax.sharding import PartitionSpec as P

D_HEAD = 128
EPSILON = 1e-06
BOTH = ("enc", "dp")
CHUNKS = (8, 8)
PER_STEP = 2
PIECES = 4
LANES = 128
EXTRA = 8
FAR_FIRST = (2, 1, -1)
F32 = jnp.float32
BF16 = jnp.bfloat16
ROWS = (((0,), (0,)), ((), ()))
COLS = (((1,), (1,)), ((), ()))


def mm(a, b, dims=(((1,), (0,)), ((), ()))):
    return lax.dot_general(a, b, dims, preferred_element_type=F32)


def mean(value):
    return jnp.mean(value, axis=-1, keepdims=True)


def attention_kernel(first, *refs):
    x_refs, (q_ref, do_ref, w_ref) = refs[:PIECES], refs[PIECES : PIECES + 3]
    acc_in = None if first else refs[PIECES + 3]
    att_ref, dq_ref, *part_refs, dw_ref, acc = refs[PIECES + (3 if first else 6) :]
    step = pl.program_id(0)
    inverse = 1.0 / math.sqrt(D_HEAD)
    per_step, span, cols = q_ref.shape
    pairs, rows, width = x_refs[0].shape
    knb = pairs // per_step
    heads = cols // D_HEAD

    @pl.when(step == 0)
    def _():
        acc[...] = jnp.zeros_like(acc) if first else acc_in[...]

    heads_at = [slice(h * D_HEAD, (h + 1) * D_HEAD) for h in range(heads)]
    each = lambda f, *lists: [f(*parts) for parts in zip(*lists)]
    x = jnp.concatenate(
        [ref[s * knb : (s + 1) * knb].reshape(knb * rows, width) for s in range(per_step) for ref in x_refs], axis=0
    )
    count = knb * rows * len(x_refs)
    spans = [slice(s * count, (s + 1) * count) for s in range(per_step)]
    both = [(s, at) for s in range(per_step) for at in heads_at]
    queries = [q_ref[s, :, at].astype(F32) for s, at in both]
    grads = [do_ref[s, :, at] for s, at in both]
    query_scales = each(lambda q: lax.rsqrt(mean(q * q) + EPSILON), queries)
    query_units = each(lambda q, c: q * c, queries, query_scales)
    query_bfs = each(lambda u: u.astype(BF16), query_units)
    keys_all = mm(x, w_ref[:, :cols]).astype(BF16).astype(F32)
    keys = [keys_all[spans[s], at] for s, at in both]
    key_scales = each(lambda k: lax.rsqrt(mean(k * k) + EPSILON), keys)
    key_units = each(lambda k, c: k * c, keys, key_scales)
    key_bfs = each(lambda u: u.astype(BF16), key_units)
    values_all = mm(x, w_ref[:, cols:]).astype(BF16)
    values = [values_all[spans[s], at] for s, at in both]
    raised = each(lambda q, k: jnp.exp(mm(q, k, COLS) * inverse), query_bfs, key_bfs)
    d_probs = each(lambda g, v: mm(g, v, COLS), grads, values)
    weights = each(lambda e: e * (1.0 / jnp.sum(e, axis=-1, keepdims=True)), raised)
    probs = each(lambda p: p.astype(BF16), weights)
    attended = each(lambda p, v: mm(p, v).astype(BF16), probs, values)
    d_values = each(lambda p, g: mm(p, g, ROWS).astype(BF16), probs, grads)
    d_scores = each(
        lambda p, d: (p * (d - jnp.sum(d * p, axis=-1, keepdims=True)) * inverse).astype(BF16), weights, d_probs
    )
    d_query_units = each(lambda d, k: mm(d, k), d_scores, key_bfs)
    d_key_units = each(lambda d, q: mm(d, q, ROWS), d_scores, query_bfs)
    d_queries = each(
        lambda c, d, u: (c * (d - u * mean(d * u))).astype(BF16), query_scales, d_query_units, query_units
    )
    d_keys = each(lambda c, d, u: (c * (d - u * mean(d * u))).astype(BF16), key_scales, d_key_units, key_units)
    d_kv = []
    for s in range(per_step):
        mine = slice(s * heads, (s + 1) * heads)
        att_ref[s] = jnp.concatenate(attended[mine], axis=1)
        dq_ref[s] = jnp.concatenate(d_queries[mine], axis=1)
        d_kv.append(jnp.concatenate(d_keys[mine] + d_values[mine], axis=1))
    d_kv = jnp.concatenate(d_kv, axis=0)
    part = mm(d_kv, w_ref[...], COLS).astype(BF16)
    for s in range(per_step):
        for i, ref in enumerate(part_refs):
            at = s * count + i * knb * rows
            ref[s * knb : (s + 1) * knb] = part[at : at + knb * rows].reshape(knb, rows, width)
    acc[...] += mm(x, d_kv, ROWS)

    @pl.when(step == pl.num_programs(0) - 1)
    def _():
        dw_ref[...] = acc[...].astype(dw_ref.dtype)


def attention(chunk, pieces, queries, d_out, w, carried):
    _, span, cols = queries.shape
    pairs, rows, width = pieces[0].shape
    mine = CHUNKS[chunk]
    knb = pairs // mine
    steps = mine // PER_STEP
    first, last = chunk == 0, chunk == len(CHUNKS) - 1
    offset = sum(CHUNKS[:chunk]) // PER_STEP
    by_stretch = pl.BlockSpec((PER_STEP, span, cols), lambda i: (offset + i, 0, 0))
    by_pair = pl.BlockSpec((PER_STEP * knb, rows, width), lambda i: (i, 0, 0))
    whole = pl.BlockSpec(w.shape, lambda i: (0, 0))
    in_specs = [by_pair] * PIECES + [by_stretch] * 2 + [whole]
    args = [*pieces, queries, d_out, w]
    aliases = {}
    if not first:
        att, dq, acc = carried
        in_specs += [whole, pl.BlockSpec(memory_space=pl.ANY), pl.BlockSpec(memory_space=pl.ANY)]
        args += [acc, att, dq]
        aliases = {PIECES + 4: 0, PIECES + 5: 1}
    out = pl.pallas_call(
        functools.partial(attention_kernel, first),
        grid=(steps,),
        in_specs=in_specs,
        out_specs=[by_stretch, by_stretch] + [by_pair] * PIECES + [whole],
        out_shape=[jax.ShapeDtypeStruct(queries.shape, BF16)] * 2
        + [jax.ShapeDtypeStruct((pairs, rows, width), BF16)] * PIECES
        + [jax.ShapeDtypeStruct(w.shape, BF16 if last else F32)],
        scratch_shapes=[pltpu.VMEM(w.shape, F32)],
        input_output_aliases=aliases,
        compiler_params=pltpu.CompilerParams(vmem_limit_bytes=40 * 1024 * 1024),
        cost_estimate=pl.CostEstimate(
            flops=mine * 900_000_000, bytes_accessed=mine * 800_000, transcendentals=mine * 66_000
        ),
        name="attention",
    )(*args)
    return out[2:-1], (out[0], out[1], out[-1])


def spread_kernel(x_ref, ids_ref, out_ref):
    held, rows, width = x_ref.shape
    count = held * rows
    at = lax.broadcasted_iota(jnp.int32, (count, count), 0)
    source = lax.rem(at, held) * rows + at // held
    turn = (source == lax.broadcasted_iota(jnp.int32, (count, count), 1)).astype(BF16)
    turned = mm(turn, x_ref[...].reshape(count, width)).astype(BF16).reshape(rows, held, width)
    blocks = width // LANES
    for i in range(blocks):
        out_ref[:, i * held : (i + 1) * held] = turned[:, :, i * LANES : (i + 1) * LANES]
    out_ref[:, blocks * held :] = jnp.broadcast_to(ids_ref[...], (rows, EXTRA, LANES))


def spread_rows(x, ids, tile=16):
    held, rows, width = x.shape
    lines = width // LANES * held + EXTRA
    return pl.pallas_call(
        spread_kernel,
        grid=(rows // tile,),
        in_specs=[pl.BlockSpec((held, tile, width), lambda i: (0, i, 0)), pl.BlockSpec(ids.shape, lambda i: (0, 0))],
        out_specs=pl.BlockSpec((tile, lines, LANES), lambda i: (i, 0, 0)),
        out_shape=jax.ShapeDtypeStruct((rows, lines, LANES), BF16),
        compiler_params=pltpu.CompilerParams(vmem_limit_bytes=32 * 1024 * 1024),
        name="spread_rows",
    )(x, ids)


def pick_kernel(held, ids_ref, table_ref, out_ref):
    ids = ids_ref[...]
    senders, lines, lanes = table_ref.shape
    count = senders * held
    hit = (ids == lax.broadcasted_iota(jnp.int32, (ids.shape[0], count), 1)).astype(BF16)
    blocks = [table_ref[:, at : at + held].reshape(count, lanes) for at in range(0, lines - EXTRA, held)]
    for i in range(0, len(blocks), 2):
        picked = mm(hit, jnp.concatenate(blocks[i : i + 2], axis=1))
        out_ref[:, i * lanes : (i + 2) * lanes] = picked.astype(BF16)


def pick_rows(ids, table, held, tile=256):
    senders, lines, lanes = table.shape
    width = (lines - EXTRA) // held * lanes
    wanted = ids.shape[0]
    return pl.pallas_call(
        functools.partial(pick_kernel, held),
        grid=(wanted // tile,),
        in_specs=[
            pl.BlockSpec((tile, 1), lambda i: (i, 0)),
            pl.BlockSpec(table.shape, lambda i: (0, 0, 0)),
        ],
        out_specs=pl.BlockSpec((tile, width), lambda i: (i, 0)),
        out_shape=jax.ShapeDtypeStruct((wanted, width), BF16),
        compiler_params=pltpu.CompilerParams(vmem_limit_bytes=48 * 1024 * 1024),
        name="pick_rows",
    )(ids.reshape(wanted, 1), table)


def place_kernel(ids_ref, rows_ref, out_ref):
    ids = ids_ref[...]
    tile = out_ref.shape[0]
    row = lax.broadcasted_iota(jnp.int32, (tile, ids.shape[1]), 0) + pl.program_id(0) * tile
    out_ref[...] = mm((ids == row).astype(BF16), rows_ref[...]).astype(BF16)


def place_rows(ids, rows, count, tile=512):
    given, width = rows.shape
    return pl.pallas_call(
        place_kernel,
        grid=(count // tile,),
        in_specs=[
            pl.BlockSpec((1, given), lambda i: (0, 0)),
            pl.BlockSpec((given, width), lambda i: (0, 0)),
        ],
        out_specs=pl.BlockSpec((tile, width), lambda i: (i, 0)),
        out_shape=jax.ShapeDtypeStruct((count, width), BF16),
        compiler_params=pltpu.CompilerParams(vmem_limit_bytes=48 * 1024 * 1024),
        name="place_rows",
    )(ids.reshape(1, given), rows)


def shift(value, by):
    count = lax.axis_size("enc")
    return lax.ppermute(value, "enc", [(i, (i + by) % count) for i in range(count)])


def gather_pieces(own):
    return [own] + [shift(own, by) for by in FAR_FIRST]


def sum_pieces(parts):
    back = [shift(part, -by) for by, part in zip(FAR_FIRST, parts[1:])]
    return sum(part.astype(F32) for part in [parts[0], *back]).astype(BF16)


def body(queries, encodings, w_key, w_value, neighbours, d_out):
    enc_count = lax.axis_size("enc")
    shards = lax.axis_size("dp")
    devices = enc_count * shards
    held, neigh_len, width = encodings.shape
    stretches, _, cols = queries.shape
    pair_count = neighbours.size
    w = jnp.concatenate([w_key, w_value], axis=1)
    blocks = width // LANES
    own_ids = neighbours.reshape(-1)
    own_ids = jnp.stack([own_ids // held, own_ids % held]).astype(BF16)
    by_row = spread_rows(encodings, jnp.pad(own_ids, ((0, EXTRA - 2), (0, LANES - pair_count))))
    table = lax.all_to_all(by_row, BOTH, 0, 0, tiled=True)
    ids = table[:shards, blocks * held : blocks * held + 2, :pair_count].astype(jnp.int32)
    ids = ids[:, 0] * held + ids[:, 1]
    knb = pair_count // stretches
    sent, start = [], 0
    for size in CHUNKS:
        wanted = ids[:, start * knb : (start + size) * knb]
        sent.append(pick_rows(wanted.reshape(-1), table, held).reshape(shards, size * knb, width))
        start += size
    pieces = []
    for c in range(len(CHUNKS)):
        if c > 0:
            sent[c], own = lax.optimization_barrier((sent[c], own))
            pieces.append(gather_pieces(own))
        own = jnp.swapaxes(lax.all_to_all(sent[c], "dp", 0, 0, tiled=True), 0, 1)
    pieces.append(gather_pieces(own))
    carried = None
    returned = []
    for c in range(len(CHUNKS)):
        parts, carried = attention(c, pieces[c], queries, d_out, w, carried)
        returned.append(sum_pieces(parts))
    att, dq, acc = carried
    d_w = lax.all_to_all(acc.reshape(shards, -1, 2 * cols), "dp", 0, 0, tiled=True)
    summed = jnp.swapaxes(jnp.concatenate(returned, axis=0), 0, 1)
    summed, d_w = lax.optimization_barrier((summed, d_w))
    rows = lax.all_to_all(summed, "dp", 0, 0, tiled=True).reshape(shards * pair_count, width)
    placed = place_rows(ids.reshape(-1), rows, devices * held).reshape(devices, held, width)
    d_encodings = jnp.swapaxes(lax.all_to_all(placed, BOTH, 0, 0, tiled=True), 0, 1)
    d_w = jnp.sum(d_w.astype(F32), axis=0)
    return att, dq, d_encodings, d_w[:, :cols], d_w[:, cols:]


def solution(mesh):
    in_specs = (
        P("dp", None, "enc"),
        P(("enc", "dp"), None, None),
        P(None, "enc"),
        P(None, "enc"),
        P("dp", None),
        P("dp", None, "enc"),
    )
    out_specs = (
        P("dp", None, "enc"),
        P("dp", None, "enc"),
        P(("enc", "dp"), None, None),
        P("dp", "enc"),
        P("dp", "enc"),
    )
    return jax.shard_map(body, mesh=mesh, in_specs=in_specs, out_specs=out_specs, check_vma=False)
```

```python
import functools
import math

import jax
import jax.numpy as jnp
from jax import lax
from jax.experimental import pallas as pl
from jax.experimental.pallas import tpu as pltpu
from jax.sharding import PartitionSpec as P

D_HEAD = 128
EPSILON = 1e-06
BOTH = ("enc", "dp")
CHUNKS = (8, 8)
PER_STEP = 2
PIECES = 4
LANES = 128
EXTRA = 8
FAR_FIRST = (2, 1, -1)
F32 = jnp.float32
BF16 = jnp.bfloat16
ROWS = (((0,), (0,)), ((), ()))
COLS = (((1,), (1,)), ((), ()))


def mm(a, b, dims=(((1,), (0,)), ((), ()))):
    return lax.dot_general(a, b, dims, preferred_element_type=F32)


def mean(value):
    return jnp.mean(value, axis=-1, keepdims=True)


def cuts(piece, rows, last):
    return [(0, rows // 2), (rows // 2, rows)] if last and piece else [(0, rows)]


def attention_kernel(first, last, *refs):
    x_refs, (q_ref, do_ref, w_ref) = refs[:PIECES], refs[PIECES : PIECES + 3]
    acc_in = None if first else refs[PIECES + 3]
    att_ref, dq_ref, *part_refs, dw_ref, acc = refs[PIECES + (3 if first else 6) :]
    step = pl.program_id(0)
    inverse = 1.0 / math.sqrt(D_HEAD)
    per_step, span, cols = q_ref.shape
    pairs, rows, width = x_refs[0].shape
    knb = pairs // per_step
    heads = cols // D_HEAD

    @pl.when(step == 0)
    def _():
        acc[...] = jnp.zeros_like(acc) if first else acc_in[...]

    heads_at = [slice(h * D_HEAD, (h + 1) * D_HEAD) for h in range(heads)]
    each = lambda f, *lists: [f(*parts) for parts in zip(*lists)]
    x = jnp.concatenate(
        [ref[s * knb : (s + 1) * knb].reshape(knb * rows, width) for s in range(per_step) for ref in x_refs], axis=0
    )
    count = knb * rows * len(x_refs)
    spans = [slice(s * count, (s + 1) * count) for s in range(per_step)]
    both = [(s, at) for s in range(per_step) for at in heads_at]
    queries = [q_ref[s, :, at].astype(F32) for s, at in both]
    grads = [do_ref[s, :, at] for s, at in both]
    query_scales = each(lambda q: lax.rsqrt(mean(q * q) + EPSILON), queries)
    query_units = each(lambda q, c: q * c, queries, query_scales)
    query_bfs = each(lambda u: u.astype(BF16), query_units)
    keys_all = mm(x, w_ref[:, :cols]).astype(BF16).astype(F32)
    keys = [keys_all[spans[s], at] for s, at in both]
    key_scales = each(lambda k: lax.rsqrt(mean(k * k) + EPSILON), keys)
    key_units = each(lambda k, c: k * c, keys, key_scales)
    key_bfs = each(lambda u: u.astype(BF16), key_units)
    values_all = mm(x, w_ref[:, cols:]).astype(BF16)
    values = [values_all[spans[s], at] for s, at in both]
    raised = each(lambda q, k: jnp.exp(mm(q, k, COLS) * inverse), query_bfs, key_bfs)
    d_probs = each(lambda g, v: mm(g, v, COLS), grads, values)
    weights = each(lambda e: e * (1.0 / jnp.sum(e, axis=-1, keepdims=True)), raised)
    probs = each(lambda p: p.astype(BF16), weights)
    attended = each(lambda p, v: mm(p, v).astype(BF16), probs, values)
    d_values = each(lambda p, g: mm(p, g, ROWS).astype(BF16), probs, grads)
    d_scores = each(
        lambda p, d: (p * (d - jnp.sum(d * p, axis=-1, keepdims=True)) * inverse).astype(BF16), weights, d_probs
    )
    d_query_units = each(lambda d, k: mm(d, k), d_scores, key_bfs)
    d_key_units = each(lambda d, q: mm(d, q, ROWS), d_scores, query_bfs)
    d_queries = each(
        lambda c, d, u: (c * (d - u * mean(d * u))).astype(BF16), query_scales, d_query_units, query_units
    )
    d_keys = each(lambda c, d, u: (c * (d - u * mean(d * u))).astype(BF16), key_scales, d_key_units, key_units)
    d_kv = []
    for s in range(per_step):
        mine = slice(s * heads, (s + 1) * heads)
        att_ref[s] = jnp.concatenate(attended[mine], axis=1)
        dq_ref[s] = jnp.concatenate(d_queries[mine], axis=1)
        d_kv.append(jnp.concatenate(d_keys[mine] + d_values[mine], axis=1))
    d_kv = jnp.concatenate(d_kv, axis=0)
    part = mm(d_kv, w_ref[...], COLS).astype(BF16)
    for s in range(per_step):
        outs = iter(part_refs)
        for i in range(PIECES):
            at = s * count + i * knb * rows
            piece = part[at : at + knb * rows].reshape(knb, rows, width)
            for low, high in cuts(i, rows, last):
                next(outs)[s * knb : (s + 1) * knb] = piece[:, low:high]
    acc[...] += mm(x, d_kv, ROWS)

    @pl.when(step == pl.num_programs(0) - 1)
    def _():
        dw_ref[...] = acc[...].astype(dw_ref.dtype)


def attention(chunk, pieces, queries, d_out, w, carried):
    _, span, cols = queries.shape
    pairs, rows, width = pieces[0].shape
    mine = CHUNKS[chunk]
    knb = pairs // mine
    steps = mine // PER_STEP
    first, last = chunk == 0, chunk == len(CHUNKS) - 1
    offset = sum(CHUNKS[:chunk]) // PER_STEP
    by_stretch = pl.BlockSpec((PER_STEP, span, cols), lambda i: (offset + i, 0, 0))
    by_pair = pl.BlockSpec((PER_STEP * knb, rows, width), lambda i: (i, 0, 0))
    whole = pl.BlockSpec(w.shape, lambda i: (0, 0))
    in_specs = [by_pair] * PIECES + [by_stretch] * 2 + [whole]
    args = [*pieces, queries, d_out, w]
    aliases = {}
    if not first:
        att, dq, acc = carried
        in_specs += [whole, pl.BlockSpec(memory_space=pl.ANY), pl.BlockSpec(memory_space=pl.ANY)]
        args += [acc, att, dq]
        aliases = {PIECES + 4: 0, PIECES + 5: 1}
    sizes = [high - low for i in range(PIECES) for low, high in cuts(i, rows, last)]
    out = pl.pallas_call(
        functools.partial(attention_kernel, first, last),
        grid=(steps,),
        in_specs=in_specs,
        out_specs=[by_stretch, by_stretch]
        + [pl.BlockSpec((PER_STEP * knb, size, width), lambda i: (i, 0, 0)) for size in sizes]
        + [whole],
        out_shape=[jax.ShapeDtypeStruct(queries.shape, BF16)] * 2
        + [jax.ShapeDtypeStruct((pairs, size, width), BF16) for size in sizes]
        + [jax.ShapeDtypeStruct(w.shape, BF16 if last else F32)],
        scratch_shapes=[pltpu.VMEM(w.shape, F32)],
        input_output_aliases=aliases,
        compiler_params=pltpu.CompilerParams(vmem_limit_bytes=40 * 1024 * 1024),
        cost_estimate=pl.CostEstimate(
            flops=mine * 900_000_000, bytes_accessed=mine * 800_000, transcendentals=mine * 66_000
        ),
        name="attention",
    )(*args)
    return out[2:-1], (out[0], out[1], out[-1])


def spread_kernel(x_ref, ids_ref, out_ref):
    held, rows, width = x_ref.shape
    count = held * rows
    at = lax.broadcasted_iota(jnp.int32, (count, count), 0)
    source = lax.rem(at, held) * rows + at // held
    turn = (source == lax.broadcasted_iota(jnp.int32, (count, count), 1)).astype(BF16)
    turned = mm(turn, x_ref[...].reshape(count, width)).astype(BF16).reshape(rows, held, width)
    blocks = width // LANES
    for i in range(blocks):
        out_ref[:, i * held : (i + 1) * held] = turned[:, :, i * LANES : (i + 1) * LANES]
    out_ref[:, blocks * held :] = jnp.broadcast_to(ids_ref[...], (rows, EXTRA, LANES))


def spread_rows(x, ids, tile=16):
    held, rows, width = x.shape
    lines = width // LANES * held + EXTRA
    return pl.pallas_call(
        spread_kernel,
        grid=(rows // tile,),
        in_specs=[pl.BlockSpec((held, tile, width), lambda i: (0, i, 0)), pl.BlockSpec(ids.shape, lambda i: (0, 0))],
        out_specs=pl.BlockSpec((tile, lines, LANES), lambda i: (i, 0, 0)),
        out_shape=jax.ShapeDtypeStruct((rows, lines, LANES), BF16),
        compiler_params=pltpu.CompilerParams(vmem_limit_bytes=32 * 1024 * 1024),
        name="spread_rows",
    )(x, ids)


def pick_kernel(held, ids_ref, table_ref, out_ref):
    ids = ids_ref[...]
    senders, lines, lanes = table_ref.shape
    count = senders * held
    hit = (ids == lax.broadcasted_iota(jnp.int32, (ids.shape[0], count), 1)).astype(BF16)
    blocks = [table_ref[:, at : at + held].reshape(count, lanes) for at in range(0, lines - EXTRA, held)]
    for i in range(0, len(blocks), 2):
        picked = mm(hit, jnp.concatenate(blocks[i : i + 2], axis=1))
        out_ref[:, i * lanes : (i + 2) * lanes] = picked.astype(BF16)


def pick_rows(ids, table, held, tile=256):
    senders, lines, lanes = table.shape
    width = (lines - EXTRA) // held * lanes
    wanted = ids.shape[0]
    return pl.pallas_call(
        functools.partial(pick_kernel, held),
        grid=(wanted // tile,),
        in_specs=[
            pl.BlockSpec((tile, 1), lambda i: (i, 0)),
            pl.BlockSpec(table.shape, lambda i: (0, 0, 0)),
        ],
        out_specs=pl.BlockSpec((tile, width), lambda i: (i, 0)),
        out_shape=jax.ShapeDtypeStruct((wanted, width), BF16),
        compiler_params=pltpu.CompilerParams(vmem_limit_bytes=48 * 1024 * 1024),
        name="pick_rows",
    )(ids.reshape(wanted, 1), table)


def place_kernel(ids_ref, rows_ref, out_ref):
    ids = ids_ref[...]
    tile = out_ref.shape[0]
    row = lax.broadcasted_iota(jnp.int32, (tile, ids.shape[1]), 0) + pl.program_id(0) * tile
    out_ref[...] = mm((ids == row).astype(BF16), rows_ref[...]).astype(BF16)


def place_rows(ids, rows, count, tile=512):
    given, width = rows.shape
    return pl.pallas_call(
        place_kernel,
        grid=(count // tile,),
        in_specs=[
            pl.BlockSpec((1, given), lambda i: (0, 0)),
            pl.BlockSpec((given, width), lambda i: (0, 0)),
        ],
        out_specs=pl.BlockSpec((tile, width), lambda i: (i, 0)),
        out_shape=jax.ShapeDtypeStruct((count, width), BF16),
        compiler_params=pltpu.CompilerParams(vmem_limit_bytes=48 * 1024 * 1024),
        name="place_rows",
    )(ids.reshape(1, given), rows)


def shift(value, by):
    count = lax.axis_size("enc")
    return lax.ppermute(value, "enc", [(i, (i + by) % count) for i in range(count)])


def gather_pieces(own):
    return [own] + [shift(own, by) for by in FAR_FIRST]


def sum_pieces(parts):
    back = [shift(part, -by) for by, part in zip(FAR_FIRST, parts[1:])]
    return sum(part.astype(F32) for part in [parts[0], *back]).astype(BF16)


def sum_halves(parts, earlier):
    own, far_a, far_b, left_a, left_b, right_a, right_b = parts
    add = lambda *terms: sum(term.astype(F32) for term in terms).astype(BF16)
    far_a, far_b = shift(far_a, 1), shift(far_b, -1)
    right_b, left_a = shift(right_b, 1), shift(left_a, -1)
    far_a, far_b, *earlier = lax.optimization_barrier((far_a, far_b, *earlier))
    right_a, left_b = shift(add(right_a, far_a), 1), shift(add(left_b, far_b), -1)
    return *earlier, add(own, jnp.concatenate([right_a, right_b], axis=1), jnp.concatenate([left_a, left_b], axis=1))


def body(queries, encodings, w_key, w_value, neighbours, d_out):
    enc_count = lax.axis_size("enc")
    shards = lax.axis_size("dp")
    devices = enc_count * shards
    held, neigh_len, width = encodings.shape
    stretches, _, cols = queries.shape
    pair_count = neighbours.size
    w = jnp.concatenate([w_key, w_value], axis=1)
    blocks = width // LANES
    own_ids = neighbours.reshape(-1)
    own_ids = jnp.stack([own_ids // held, own_ids % held]).astype(BF16)
    by_row = spread_rows(encodings, jnp.pad(own_ids, ((0, EXTRA - 2), (0, LANES - pair_count))))
    table = lax.all_to_all(by_row, BOTH, 0, 0, tiled=True)
    ids = table[:shards, blocks * held : blocks * held + 2, :pair_count].astype(jnp.int32)
    ids = ids[:, 0] * held + ids[:, 1]
    knb = pair_count // stretches
    sent, start = [], 0
    for size in CHUNKS:
        wanted = ids[:, start * knb : (start + size) * knb]
        sent.append(pick_rows(wanted.reshape(-1), table, held).reshape(shards, size * knb, width))
        start += size
    pieces = []
    for c in range(len(CHUNKS)):
        if c > 0:
            sent[c], own = lax.optimization_barrier((sent[c], own))
            pieces.append(gather_pieces(own))
        own = jnp.swapaxes(lax.all_to_all(sent[c], "dp", 0, 0, tiled=True), 0, 1)
    pieces.append(gather_pieces(own))
    carried = None
    returned = []
    for c in range(len(CHUNKS)):
        parts, carried = attention(c, pieces[c], queries, d_out, w, carried)
        if c < len(CHUNKS) - 1:
            returned.append(sum_pieces(parts))
    returned = sum_halves(parts, returned)
    att, dq, acc = carried
    d_w = lax.all_to_all(acc.reshape(shards, -1, 2 * cols), "dp", 0, 0, tiled=True)
    summed = jnp.swapaxes(jnp.concatenate(returned, axis=0), 0, 1)
    summed, d_w = lax.optimization_barrier((summed, d_w))
    rows = lax.all_to_all(summed, "dp", 0, 0, tiled=True).reshape(shards * pair_count, width)
    placed = place_rows(ids.reshape(-1), rows, devices * held).reshape(devices, held, width)
    d_encodings = jnp.swapaxes(lax.all_to_all(placed, BOTH, 0, 0, tiled=True), 0, 1)
    d_w = jnp.sum(d_w.astype(F32), axis=0)
    return att, dq, d_encodings, d_w[:, :cols], d_w[:, cols:]


def solution(mesh):
    in_specs = (
        P("dp", None, "enc"),
        P(("enc", "dp"), None, None),
        P(None, "enc"),
        P(None, "enc"),
        P("dp", None),
        P("dp", None, "enc"),
    )
    out_specs = (
        P("dp", None, "enc"),
        P("dp", None, "enc"),
        P(("enc", "dp"), None, None),
        P("dp", "enc"),
        P("dp", "enc"),
    )
    return jax.shard_map(body, mesh=mesh, in_specs=in_specs, out_specs=out_specs, check_vma=False)
```

```python
import functools
import math

import jax
import jax.numpy as jnp
from jax import lax
from jax.experimental import pallas as pl
from jax.experimental.pallas import tpu as pltpu
from jax.sharding import PartitionSpec as P

D_HEAD = 128
EPSILON = 1e-06
BOTH = ("enc", "dp")
CHUNKS = (8, 8)
PER_STEP = 4
PIECES = 4
LANES = 128
EXTRA = 8
SPREAD_TILE = 16
FAR_FIRST = (2, 1, -1)
F32 = jnp.float32
BF16 = jnp.bfloat16
ROWS = (((0,), (0,)), ((), ()))
COLS = (((1,), (1,)), ((), ()))


def mm(a, b, dims=(((1,), (0,)), ((), ()))):
    return lax.dot_general(a, b, dims, preferred_element_type=F32)


def mean(value):
    return jnp.mean(value, axis=-1, keepdims=True)


def cuts(piece, rows, last):
    return [(0, rows // 2), (rows // 2, rows)] if last and piece else [(0, rows)]


def attention_kernel(first, last, *refs):
    x_refs, (q_ref, do_ref, w_ref) = refs[:PIECES], refs[PIECES : PIECES + 3]
    acc_in = None if first else refs[PIECES + 3]
    att_ref, dq_ref, *part_refs, dw_ref, acc = refs[PIECES + (3 if first else 6) :]
    step = pl.program_id(0)
    inverse = 1.0 / math.sqrt(D_HEAD)
    per_step, span, cols = q_ref.shape
    pairs, rows, width = x_refs[0].shape
    knb = pairs // per_step
    heads = cols // D_HEAD

    @pl.when(step == 0)
    def _():
        acc[...] = jnp.zeros_like(acc) if first else acc_in[...]

    heads_at = [slice(h * D_HEAD, (h + 1) * D_HEAD) for h in range(heads)]
    each = lambda f, *lists: [f(*parts) for parts in zip(*lists)]
    x = jnp.concatenate(
        [ref[s * knb : (s + 1) * knb].reshape(knb * rows, width) for s in range(per_step) for ref in x_refs], axis=0
    )
    count = knb * rows * len(x_refs)
    spans = [slice(s * count, (s + 1) * count) for s in range(per_step)]
    both = [(s, at) for s in range(per_step) for at in heads_at]
    queries = [q_ref[s, :, at].astype(F32) for s, at in both]
    grads = [do_ref[s, :, at] for s, at in both]
    query_scales = each(lambda q: lax.rsqrt(mean(q * q) + EPSILON), queries)
    query_units = each(lambda q, c: q * c, queries, query_scales)
    query_bfs = each(lambda u: u.astype(BF16), query_units)
    keys_all = mm(x, w_ref[:, :cols]).astype(BF16).astype(F32)
    keys = [keys_all[spans[s], at] for s, at in both]
    key_scales = each(lambda k: lax.rsqrt(mean(k * k) + EPSILON), keys)
    key_units = each(lambda k, c: k * c, keys, key_scales)
    key_bfs = each(lambda u: u.astype(BF16), key_units)
    values_all = mm(x, w_ref[:, cols:]).astype(BF16)
    values = [values_all[spans[s], at] for s, at in both]
    blank = jnp.zeros((span, D_HEAD), BF16)
    rows_of = lambda top, bottom: jnp.concatenate([top, bottom], axis=0)
    cols_of = lambda left, right: jnp.concatenate([left, right], axis=1)
    outer = each(lambda q, g: rows_of(cols_of(q, blank), cols_of(blank, g)), query_bfs, grads)
    inner = each(cols_of, key_bfs, values)
    products = each(lambda o, i: mm(o, i, COLS), outer, inner)
    raised = each(lambda p: jnp.exp(p[:span] * inverse), products)
    d_probs = each(lambda p: p[span:], products)
    weights = each(lambda e: e * (1.0 / jnp.sum(e, axis=-1, keepdims=True)), raised)
    probs = each(lambda p: p.astype(BF16), weights)
    d_scores = each(
        lambda p, d: (p * (d - jnp.sum(d * p, axis=-1, keepdims=True)) * inverse).astype(BF16), weights, d_probs
    )
    middle = each(rows_of, d_scores, probs)
    to_queries = each(mm, middle, inner)
    to_keys = each(lambda m, o: mm(m, o, ROWS), middle, outer)
    d_query_units = each(lambda t: t[:span, :D_HEAD], to_queries)
    attended = each(lambda t: t[span:, D_HEAD:].astype(BF16), to_queries)
    d_key_units = each(lambda t: t[:, :D_HEAD], to_keys)
    d_values = each(lambda t: t[:, D_HEAD:].astype(BF16), to_keys)
    d_queries = each(
        lambda c, d, u: (c * (d - u * mean(d * u))).astype(BF16), query_scales, d_query_units, query_units
    )
    d_keys = each(lambda c, d, u: (c * (d - u * mean(d * u))).astype(BF16), key_scales, d_key_units, key_units)
    d_kv = []
    for s in range(per_step):
        mine = slice(s * heads, (s + 1) * heads)
        att_ref[s] = jnp.concatenate(attended[mine], axis=1)
        dq_ref[s] = jnp.concatenate(d_queries[mine], axis=1)
        d_kv.append(jnp.concatenate(d_keys[mine] + d_values[mine], axis=1))
    d_kv = jnp.concatenate(d_kv, axis=0)
    part = mm(d_kv, w_ref[...], COLS).astype(BF16)
    for s in range(per_step):
        outs = iter(part_refs)
        for i in range(PIECES):
            at = s * count + i * knb * rows
            piece = part[at : at + knb * rows].reshape(knb, rows, width)
            for low, high in cuts(i, rows, last):
                next(outs)[s * knb : (s + 1) * knb] = piece[:, low:high]
    acc[...] += mm(x, d_kv, ROWS)

    @pl.when(step == pl.num_programs(0) - 1)
    def _():
        dw_ref[...] = acc[...].astype(dw_ref.dtype)


def attention(chunk, pieces, queries, d_out, w, carried):
    _, span, cols = queries.shape
    pairs, rows, width = pieces[0].shape
    mine = CHUNKS[chunk]
    knb = pairs // mine
    steps = mine // PER_STEP
    first, last = chunk == 0, chunk == len(CHUNKS) - 1
    offset = sum(CHUNKS[:chunk]) // PER_STEP
    by_stretch = pl.BlockSpec((PER_STEP, span, cols), lambda i: (offset + i, 0, 0))
    by_pair = pl.BlockSpec((PER_STEP * knb, rows, width), lambda i: (i, 0, 0))
    whole = pl.BlockSpec(w.shape, lambda i: (0, 0))
    in_specs = [by_pair] * PIECES + [by_stretch] * 2 + [whole]
    args = [*pieces, queries, d_out, w]
    aliases = {}
    if not first:
        att, dq, acc = carried
        in_specs += [whole, pl.BlockSpec(memory_space=pl.ANY), pl.BlockSpec(memory_space=pl.ANY)]
        args += [acc, att, dq]
        aliases = {PIECES + 4: 0, PIECES + 5: 1}
    sizes = [high - low for i in range(PIECES) for low, high in cuts(i, rows, last)]
    out = pl.pallas_call(
        functools.partial(attention_kernel, first, last),
        grid=(steps,),
        in_specs=in_specs,
        out_specs=[by_stretch, by_stretch]
        + [pl.BlockSpec((PER_STEP * knb, size, width), lambda i: (i, 0, 0)) for size in sizes]
        + [whole],
        out_shape=[jax.ShapeDtypeStruct(queries.shape, BF16)] * 2
        + [jax.ShapeDtypeStruct((pairs, size, width), BF16) for size in sizes]
        + [jax.ShapeDtypeStruct(w.shape, BF16 if last else F32)],
        scratch_shapes=[pltpu.VMEM(w.shape, F32)],
        input_output_aliases=aliases,
        compiler_params=pltpu.CompilerParams(vmem_limit_bytes=40 * 1024 * 1024),
        cost_estimate=pl.CostEstimate(
            flops=mine * 900_000_000, bytes_accessed=mine * 800_000, transcendentals=mine * 66_000
        ),
        name="attention",
    )(*args)
    return out[2:-1], (out[0], out[1], out[-1])


def spread_kernel(x_ref, ids_ref, out_ref):
    held, rows, width = x_ref.shape
    count = held * SPREAD_TILE
    at = lax.broadcasted_iota(jnp.int32, (count, count), 0)
    source = lax.rem(at, held) * SPREAD_TILE + at // held
    turn = (source == lax.broadcasted_iota(jnp.int32, (count, count), 1)).astype(BF16)
    blocks = width // LANES
    out_ref[:, blocks * held :] = jnp.broadcast_to(ids_ref[...], (rows, EXTRA, LANES))
    for r in range(0, rows, SPREAD_TILE):
        turned = mm(turn, x_ref[:, r : r + SPREAD_TILE].reshape(count, width)).astype(BF16)
        turned = turned.reshape(SPREAD_TILE, held, width)
        for i in range(blocks):
            out_ref[r : r + SPREAD_TILE, i * held : (i + 1) * held] = turned[:, :, i * LANES : (i + 1) * LANES]


def spread_rows(x, ids):
    held, rows, width = x.shape
    lines = width // LANES * held + EXTRA
    return pl.pallas_call(
        spread_kernel,
        in_specs=[pl.BlockSpec(memory_space=pltpu.VMEM)] * 2,
        out_specs=pl.BlockSpec(memory_space=pltpu.VMEM),
        out_shape=jax.ShapeDtypeStruct((rows, lines, LANES), BF16),
        compiler_params=pltpu.CompilerParams(vmem_limit_bytes=32 * 1024 * 1024),
        name="spread_rows",
    )(x, ids)


def pick_kernel(held, ids_ref, table_ref, out_ref):
    ids = ids_ref[...]
    senders, lines, lanes = table_ref.shape
    count = senders * held
    hit = (ids == lax.broadcasted_iota(jnp.int32, (ids.shape[0], count), 1)).astype(BF16)
    blocks = [table_ref[:, at : at + held].reshape(count, lanes) for at in range(0, lines - EXTRA, held)]
    for i in range(0, len(blocks), 2):
        picked = mm(hit, jnp.concatenate(blocks[i : i + 2], axis=1))
        out_ref[:, i * lanes : (i + 2) * lanes] = picked.astype(BF16)


def pick_rows(ids, table, held):
    senders, lines, lanes = table.shape
    width = (lines - EXTRA) // held * lanes
    return pl.pallas_call(
        functools.partial(pick_kernel, held),
        in_specs=[pl.BlockSpec(memory_space=pltpu.VMEM)] * 2,
        out_specs=pl.BlockSpec(memory_space=pltpu.VMEM),
        out_shape=jax.ShapeDtypeStruct((ids.shape[0], width), BF16),
        compiler_params=pltpu.CompilerParams(vmem_limit_bytes=32 * 1024 * 1024),
        name="pick_rows",
    )(ids.reshape(-1, 1), table)


def place_kernel(ids_ref, rows_ref, out_ref):
    ids = ids_ref[...]
    tile = out_ref.shape[0]
    row = lax.broadcasted_iota(jnp.int32, (tile, ids.shape[1]), 0) + pl.program_id(0) * tile
    out_ref[...] = mm((ids == row).astype(BF16), rows_ref[...]).astype(BF16)


def place_rows(ids, rows, count, tile=512):
    given, width = rows.shape
    return pl.pallas_call(
        place_kernel,
        grid=(count // tile,),
        in_specs=[
            pl.BlockSpec((1, given), lambda i: (0, 0)),
            pl.BlockSpec((given, width), lambda i: (0, 0)),
        ],
        out_specs=pl.BlockSpec((tile, width), lambda i: (i, 0)),
        out_shape=jax.ShapeDtypeStruct((count, width), BF16),
        compiler_params=pltpu.CompilerParams(vmem_limit_bytes=48 * 1024 * 1024),
        name="place_rows",
    )(ids.reshape(1, given), rows)


def shift(value, by):
    count = lax.axis_size("enc")
    return lax.ppermute(value, "enc", [(i, (i + by) % count) for i in range(count)])


def gather_pieces(own):
    return [own] + [shift(own, by) for by in FAR_FIRST]


def sum_pieces(parts):
    back = [shift(part, -by) for by, part in zip(FAR_FIRST, parts[1:])]
    return sum(part.astype(F32) for part in [parts[0], *back]).astype(BF16)


def sum_halves(parts, earlier):
    own, far_a, far_b, left_a, left_b, right_a, right_b = parts
    add = lambda *terms: sum(term.astype(F32) for term in terms).astype(BF16)
    far_a, far_b = shift(far_a, 1), shift(far_b, -1)
    right_b, left_a = shift(right_b, 1), shift(left_a, -1)
    far_a, far_b, *earlier = lax.optimization_barrier((far_a, far_b, *earlier))
    right_a, left_b = shift(add(right_a, far_a), 1), shift(add(left_b, far_b), -1)
    return *earlier, add(own, jnp.concatenate([right_a, right_b], axis=1), jnp.concatenate([left_a, left_b], axis=1))


def body(queries, encodings, w_key, w_value, neighbours, d_out):
    enc_count = lax.axis_size("enc")
    shards = lax.axis_size("dp")
    devices = enc_count * shards
    held, neigh_len, width = encodings.shape
    stretches, _, cols = queries.shape
    pair_count = neighbours.size
    w = jnp.concatenate([w_key, w_value], axis=1)
    blocks = width // LANES
    own_ids = neighbours.reshape(-1)
    own_ids = jnp.stack([own_ids // held, own_ids % held]).astype(BF16)
    by_row = spread_rows(encodings, jnp.pad(own_ids, ((0, EXTRA - 2), (0, LANES - pair_count))))
    table = lax.all_to_all(by_row, BOTH, 0, 0, tiled=True)
    ids = table[:shards, blocks * held : blocks * held + 2, :pair_count].astype(jnp.int32)
    ids = ids[:, 0] * held + ids[:, 1]
    knb = pair_count // stretches
    sent, start = [], 0
    for size in CHUNKS:
        wanted = ids[:, start * knb : (start + size) * knb]
        sent.append(pick_rows(wanted.reshape(-1), table, held).reshape(shards, size * knb, width))
        start += size
    pieces = []
    for c in range(len(CHUNKS)):
        if c > 0:
            sent[c], own = lax.optimization_barrier((sent[c], own))
            pieces.append(gather_pieces(own))
        own = jnp.swapaxes(lax.all_to_all(sent[c], "dp", 0, 0, tiled=True), 0, 1)
    pieces.append(gather_pieces(own))
    carried = None
    returned = []
    for c in range(len(CHUNKS)):
        parts, carried = attention(c, pieces[c], queries, d_out, w, carried)
        if c < len(CHUNKS) - 1:
            returned.append(sum_pieces(parts))
    returned = sum_halves(parts, returned)
    att, dq, acc = carried
    d_w = lax.all_to_all(acc.reshape(shards, -1, 2 * cols), "dp", 0, 0, tiled=True)
    summed = jnp.swapaxes(jnp.concatenate(returned, axis=0), 0, 1)
    summed, d_w = lax.optimization_barrier((summed, d_w))
    rows = lax.all_to_all(summed, "dp", 0, 0, tiled=True).reshape(shards * pair_count, width)
    placed = place_rows(ids.reshape(-1), rows, devices * held).reshape(devices, held, width)
    d_encodings = jnp.swapaxes(lax.all_to_all(placed, BOTH, 0, 0, tiled=True), 0, 1)
    d_w = jnp.sum(d_w.astype(F32), axis=0)
    return att, dq, d_encodings, d_w[:, :cols], d_w[:, cols:]


def solution(mesh):
    in_specs = (
        P("dp", None, "enc"),
        P(("enc", "dp"), None, None),
        P(None, "enc"),
        P(None, "enc"),
        P("dp", None),
        P("dp", None, "enc"),
    )
    out_specs = (
        P("dp", None, "enc"),
        P("dp", None, "enc"),
        P(("enc", "dp"), None, None),
        P("dp", "enc"),
        P("dp", "enc"),
    )
    return jax.shard_map(body, mesh=mesh, in_specs=in_specs, out_specs=out_specs, check_vma=False)
```

```python
import functools
import math

import jax
import jax.numpy as jnp
from jax import lax
from jax.experimental import pallas as pl
from jax.experimental.pallas import tpu as pltpu
from jax.sharding import PartitionSpec as P

D_HEAD = 128
EPSILON = 1e-06
BOTH = ("enc", "dp")
CHUNKS = (8, 8)
PER_STEP = 4
PIECES = 4
LANES = 128
EXTRA = 8
SPREAD_TILE = 16
PLACE_TILE = 512
FAR_FIRST = (2, 1, -1)
F32 = jnp.float32
BF16 = jnp.bfloat16
ROWS = (((0,), (0,)), ((), ()))
COLS = (((1,), (1,)), ((), ()))


def mm(a, b, dims=(((1,), (0,)), ((), ()))):
    return lax.dot_general(a, b, dims, preferred_element_type=F32)


def mean(value):
    return jnp.mean(value, axis=-1, keepdims=True)


def cuts(piece, rows, last):
    return [(0, rows // 2), (rows // 2, rows)] if last and piece else [(0, rows)]


def attention_kernel(first, last, *refs):
    x_refs, (q_ref, do_ref, w_ref) = refs[:PIECES], refs[PIECES : PIECES + 3]
    acc_in = None if first else refs[PIECES + 3]
    att_ref, dq_ref, *part_refs, dw_ref, acc = refs[PIECES + (3 if first else 6) :]
    step = pl.program_id(0)
    inverse = 1.0 / math.sqrt(D_HEAD)
    per_step, span, cols = q_ref.shape
    pairs, rows, width = x_refs[0].shape
    knb = pairs // per_step
    heads = cols // D_HEAD

    @pl.when(step == 0)
    def _():
        acc[...] = jnp.zeros_like(acc) if first else acc_in[...]

    heads_at = [slice(h * D_HEAD, (h + 1) * D_HEAD) for h in range(heads)]
    each = lambda f, *lists: [f(*parts) for parts in zip(*lists)]
    x = jnp.concatenate(
        [ref[s * knb : (s + 1) * knb].reshape(knb * rows, width) for s in range(per_step) for ref in x_refs], axis=0
    )
    count = knb * rows * len(x_refs)
    spans = [slice(s * count, (s + 1) * count) for s in range(per_step)]
    both = [(s, at) for s in range(per_step) for at in heads_at]
    queries = [q_ref[s, :, at].astype(F32) for s, at in both]
    grads = [do_ref[s, :, at] for s, at in both]
    query_scales = each(lambda q: lax.rsqrt(mean(q * q) + EPSILON), queries)
    query_units = each(lambda q, c: q * c, queries, query_scales)
    query_bfs = each(lambda u: u.astype(BF16), query_units)
    keys_all = mm(x, w_ref[:, :cols]).astype(BF16).astype(F32)
    keys = [keys_all[spans[s], at] for s, at in both]
    key_scales = each(lambda k: lax.rsqrt(mean(k * k) + EPSILON), keys)
    key_units = each(lambda k, c: k * c, keys, key_scales)
    key_bfs = each(lambda u: u.astype(BF16), key_units)
    values_all = mm(x, w_ref[:, cols:]).astype(BF16)
    values = [values_all[spans[s], at] for s, at in both]
    blank = jnp.zeros((span, D_HEAD), BF16)
    rows_of = lambda top, bottom: jnp.concatenate([top, bottom], axis=0)
    cols_of = lambda left, right: jnp.concatenate([left, right], axis=1)
    outer = each(lambda q, g: rows_of(cols_of(q, blank), cols_of(blank, g)), query_bfs, grads)
    inner = each(cols_of, key_bfs, values)
    products = each(lambda o, i: mm(o, i, COLS), outer, inner)
    raised = each(lambda p: jnp.exp(p[:span] * inverse), products)
    d_probs = each(lambda p: p[span:], products)
    weights = each(lambda e: e * (1.0 / jnp.sum(e, axis=-1, keepdims=True)), raised)
    probs = each(lambda p: p.astype(BF16), weights)
    d_scores = each(
        lambda p, d: (p * (d - jnp.sum(d * p, axis=-1, keepdims=True)) * inverse).astype(BF16), weights, d_probs
    )
    middle = each(rows_of, d_scores, probs)
    to_queries = each(mm, middle, inner)
    to_keys = each(lambda m, o: mm(m, o, ROWS), middle, outer)
    d_query_units = each(lambda t: t[:span, :D_HEAD], to_queries)
    attended = each(lambda t: t[span:, D_HEAD:].astype(BF16), to_queries)
    d_key_units = each(lambda t: t[:, :D_HEAD], to_keys)
    d_values = each(lambda t: t[:, D_HEAD:].astype(BF16), to_keys)
    d_queries = each(
        lambda c, d, u: (c * (d - u * mean(d * u))).astype(BF16), query_scales, d_query_units, query_units
    )
    d_keys = each(lambda c, d, u: (c * (d - u * mean(d * u))).astype(BF16), key_scales, d_key_units, key_units)
    d_kv = []
    for s in range(per_step):
        mine = slice(s * heads, (s + 1) * heads)
        att_ref[s] = jnp.concatenate(attended[mine], axis=1)
        dq_ref[s] = jnp.concatenate(d_queries[mine], axis=1)
        d_kv.append(jnp.concatenate(d_keys[mine] + d_values[mine], axis=1))
    d_kv = jnp.concatenate(d_kv, axis=0)
    part = mm(d_kv, w_ref[...], COLS).astype(BF16)
    for s in range(per_step):
        outs = iter(part_refs)
        for i in range(PIECES):
            at = s * count + i * knb * rows
            piece = part[at : at + knb * rows].reshape(knb, rows, width)
            for low, high in cuts(i, rows, last):
                next(outs)[s * knb : (s + 1) * knb] = piece[:, low:high]
    acc[...] += mm(x, d_kv, ROWS)

    @pl.when(step == pl.num_programs(0) - 1)
    def _():
        dw_ref[...] = acc[...].astype(dw_ref.dtype)


def attention(chunk, pieces, queries, d_out, w, carried):
    _, span, cols = queries.shape
    pairs, rows, width = pieces[0].shape
    mine = CHUNKS[chunk]
    knb = pairs // mine
    steps = mine // PER_STEP
    first, last = chunk == 0, chunk == len(CHUNKS) - 1
    offset = sum(CHUNKS[:chunk]) // PER_STEP
    by_stretch = pl.BlockSpec((PER_STEP, span, cols), lambda i: (offset + i, 0, 0))
    by_pair = pl.BlockSpec((PER_STEP * knb, rows, width), lambda i: (i, 0, 0))
    whole = pl.BlockSpec(w.shape, lambda i: (0, 0))
    in_specs = [by_pair] * PIECES + [by_stretch] * 2 + [whole]
    args = [*pieces, queries, d_out, w]
    aliases = {}
    if not first:
        att, dq, acc = carried
        in_specs += [whole, pl.BlockSpec(memory_space=pl.ANY), pl.BlockSpec(memory_space=pl.ANY)]
        args += [acc, att, dq]
        aliases = {PIECES + 4: 0, PIECES + 5: 1}
    sizes = [high - low for i in range(PIECES) for low, high in cuts(i, rows, last)]
    out = pl.pallas_call(
        functools.partial(attention_kernel, first, last),
        grid=(steps,),
        in_specs=in_specs,
        out_specs=[by_stretch, by_stretch]
        + [pl.BlockSpec((PER_STEP * knb, size, width), lambda i: (i, 0, 0)) for size in sizes]
        + [whole],
        out_shape=[jax.ShapeDtypeStruct(queries.shape, BF16)] * 2
        + [jax.ShapeDtypeStruct((pairs, size, width), BF16) for size in sizes]
        + [jax.ShapeDtypeStruct(w.shape, BF16 if last else F32)],
        scratch_shapes=[pltpu.VMEM(w.shape, F32)],
        input_output_aliases=aliases,
        compiler_params=pltpu.CompilerParams(vmem_limit_bytes=40 * 1024 * 1024),
        cost_estimate=pl.CostEstimate(
            flops=mine * 900_000_000, bytes_accessed=mine * 800_000, transcendentals=mine * 66_000
        ),
        name="attention",
    )(*args)
    return out[2:-1], (out[0], out[1], out[-1])


def spread_kernel(x_ref, ids_ref, out_ref):
    held, rows, width = x_ref.shape
    count = held * SPREAD_TILE
    at = lax.broadcasted_iota(jnp.int32, (count, count), 0)
    source = lax.rem(at, held) * SPREAD_TILE + at // held
    turn = (source == lax.broadcasted_iota(jnp.int32, (count, count), 1)).astype(BF16)
    blocks = width // LANES
    out_ref[:, blocks * held :] = jnp.broadcast_to(ids_ref[...], (rows, EXTRA, LANES))
    for r in range(0, rows, SPREAD_TILE):
        turned = mm(turn, x_ref[:, r : r + SPREAD_TILE].reshape(count, width)).astype(BF16)
        turned = turned.reshape(SPREAD_TILE, held, width)
        for i in range(blocks):
            out_ref[r : r + SPREAD_TILE, i * held : (i + 1) * held] = turned[:, :, i * LANES : (i + 1) * LANES]


def spread_rows(x, ids):
    held, rows, width = x.shape
    lines = width // LANES * held + EXTRA
    return pl.pallas_call(
        spread_kernel,
        in_specs=[pl.BlockSpec(memory_space=pltpu.VMEM)] * 2,
        out_specs=pl.BlockSpec(memory_space=pltpu.VMEM),
        out_shape=jax.ShapeDtypeStruct((rows, lines, LANES), BF16),
        compiler_params=pltpu.CompilerParams(vmem_limit_bytes=32 * 1024 * 1024),
        name="spread_rows",
    )(x, ids)


def pick_first_kernel(held, shards, first, table_ref, out_ref):
    senders, lines, lanes = table_ref.shape
    count, wanted = senders * held, out_ref.shape[0]
    each = wanted // shards
    ends = table_ref[:shards, lines - EXTRA :].astype(F32)
    row = lax.broadcasted_iota(jnp.int32, (wanted, shards), 0)
    owner = (row // each == lax.broadcasted_iota(jnp.int32, (wanted, shards), 1)).astype(BF16)
    high, low = (mm(owner, ends[:, i].astype(BF16)) for i in range(2))
    lane = lax.broadcasted_iota(jnp.int32, (wanted, lanes), 1)
    mine = lane == lax.rem(lax.broadcasted_iota(jnp.int32, (wanted, lanes), 0), each) + first
    ids = jnp.sum(jnp.where(mine, high * held + low, 0.0), axis=-1, keepdims=True).astype(jnp.int32)
    hit = (ids == lax.broadcasted_iota(jnp.int32, (wanted, count), 1)).astype(BF16)
    blocks = [table_ref[:, at : at + held].reshape(count, lanes) for at in range(0, lines - EXTRA, held)]
    for i in range(0, len(blocks), 2):
        picked = mm(hit, jnp.concatenate(blocks[i : i + 2], axis=1))
        out_ref[:, i * lanes : (i + 2) * lanes] = picked.astype(BF16)


def pick_first_rows(table, held, shards, first, each):
    senders, lines, lanes = table.shape
    width = (lines - EXTRA) // held * lanes
    return pl.pallas_call(
        functools.partial(pick_first_kernel, held, shards, first),
        in_specs=[pl.BlockSpec(memory_space=pltpu.VMEM)],
        out_specs=pl.BlockSpec(memory_space=pltpu.VMEM),
        out_shape=jax.ShapeDtypeStruct((shards * each, width), BF16),
        compiler_params=pltpu.CompilerParams(vmem_limit_bytes=32 * 1024 * 1024),
        name="pick_first_rows",
    )(table)


def pick_kernel(held, ids_ref, table_ref, out_ref):
    ids = ids_ref[...]
    senders, lines, lanes = table_ref.shape
    count = senders * held
    hit = (ids == lax.broadcasted_iota(jnp.int32, (ids.shape[0], count), 1)).astype(BF16)
    blocks = [table_ref[:, at : at + held].reshape(count, lanes) for at in range(0, lines - EXTRA, held)]
    for i in range(0, len(blocks), 2):
        picked = mm(hit, jnp.concatenate(blocks[i : i + 2], axis=1))
        out_ref[:, i * lanes : (i + 2) * lanes] = picked.astype(BF16)


def pick_rows(ids, table, held):
    senders, lines, lanes = table.shape
    width = (lines - EXTRA) // held * lanes
    return pl.pallas_call(
        functools.partial(pick_kernel, held),
        in_specs=[pl.BlockSpec(memory_space=pltpu.VMEM)] * 2,
        out_specs=pl.BlockSpec(memory_space=pltpu.VMEM),
        out_shape=jax.ShapeDtypeStruct((ids.shape[0], width), BF16),
        compiler_params=pltpu.CompilerParams(vmem_limit_bytes=32 * 1024 * 1024),
        name="pick_rows",
    )(ids.reshape(-1, 1), table)


def place_kernel(ids_ref, rows_ref, out_ref):
    ids = ids_ref[...]
    for at in range(0, out_ref.shape[0], PLACE_TILE):
        row = lax.broadcasted_iota(jnp.int32, (PLACE_TILE, ids.shape[1]), 0) + at
        out_ref[at : at + PLACE_TILE] = mm((ids == row).astype(BF16), rows_ref[...]).astype(BF16)


def place_rows(ids, rows, count):
    return pl.pallas_call(
        place_kernel,
        in_specs=[pl.BlockSpec(memory_space=pltpu.VMEM)] * 2,
        out_specs=pl.BlockSpec(memory_space=pltpu.VMEM),
        out_shape=jax.ShapeDtypeStruct((count, rows.shape[1]), BF16),
        compiler_params=pltpu.CompilerParams(vmem_limit_bytes=32 * 1024 * 1024),
        name="place_rows",
    )(ids.reshape(1, -1), rows)


def shift(value, by):
    count = lax.axis_size("enc")
    return lax.ppermute(value, "enc", [(i, (i + by) % count) for i in range(count)])


def gather_pieces(own):
    return [own] + [shift(own, by) for by in FAR_FIRST]


def sum_pieces(parts):
    back = [shift(part, -by) for by, part in zip(FAR_FIRST, parts[1:])]
    return sum(part.astype(F32) for part in [parts[0], *back]).astype(BF16)


def sum_halves(parts, earlier):
    own, far_a, far_b, left_a, left_b, right_a, right_b = parts
    add = lambda *terms: sum(term.astype(F32) for term in terms).astype(BF16)
    far_a, far_b = shift(far_a, 1), shift(far_b, -1)
    right_b, left_a = shift(right_b, 1), shift(left_a, -1)
    far_a, far_b, *earlier = lax.optimization_barrier((far_a, far_b, *earlier))
    right_a, left_b = shift(add(right_a, far_a), 1), shift(add(left_b, far_b), -1)
    return *earlier, add(own, jnp.concatenate([right_a, right_b], axis=1), jnp.concatenate([left_a, left_b], axis=1))


def body(queries, encodings, w_key, w_value, neighbours, d_out):
    enc_count = lax.axis_size("enc")
    shards = lax.axis_size("dp")
    devices = enc_count * shards
    held, neigh_len, width = encodings.shape
    stretches, _, cols = queries.shape
    pair_count = neighbours.size
    w = jnp.concatenate([w_key, w_value], axis=1)
    blocks = width // LANES
    own_ids = neighbours.reshape(-1)
    own_ids = jnp.stack([own_ids // held, own_ids % held]).astype(BF16)
    by_row = spread_rows(encodings, jnp.pad(own_ids, ((0, EXTRA - 2), (0, LANES - pair_count))))
    table = lax.all_to_all(by_row, BOTH, 0, 0, tiled=True)
    ids = table[:shards, blocks * held : blocks * held + 2, :pair_count].astype(jnp.int32)
    ids = ids[:, 0] * held + ids[:, 1]
    knb = pair_count // stretches
    sent, start = [], 0
    for size in CHUNKS:
        if start == 0:
            sent.append(pick_first_rows(table, held, shards, 0, size * knb))
        else:
            wanted = ids[:, start * knb : (start + size) * knb]
            sent.append(pick_rows(wanted.reshape(-1), table, held))
        sent[-1] = sent[-1].reshape(shards, size * knb, width)
        start += size
    pieces = []
    for c in range(len(CHUNKS)):
        if c > 0:
            sent[c], own = lax.optimization_barrier((sent[c], own))
            pieces.append(gather_pieces(own))
        own = jnp.swapaxes(lax.all_to_all(sent[c], "dp", 0, 0, tiled=True), 0, 1)
    pieces.append(gather_pieces(own))
    carried = None
    returned = []
    for c in range(len(CHUNKS)):
        parts, carried = attention(c, pieces[c], queries, d_out, w, carried)
        if c < len(CHUNKS) - 1:
            returned.append(sum_pieces(parts))
    returned = sum_halves(parts, returned)
    att, dq, acc = carried
    d_w = lax.all_to_all(acc.reshape(shards, -1, 2 * cols), "dp", 0, 0, tiled=True)
    summed = jnp.swapaxes(jnp.concatenate(returned, axis=0), 0, 1)
    summed, d_w = lax.optimization_barrier((summed, d_w))
    rows = lax.all_to_all(summed, "dp", 0, 0, tiled=True).reshape(shards * pair_count, width)
    placed = place_rows(ids.reshape(-1), rows, devices * held).reshape(devices, held, width)
    d_encodings = jnp.swapaxes(lax.all_to_all(placed, BOTH, 0, 0, tiled=True), 0, 1)
    d_w = jnp.sum(d_w.astype(F32), axis=0)
    return att, dq, d_encodings, d_w[:, :cols], d_w[:, cols:]


def solution(mesh):
    in_specs = (
        P("dp", None, "enc"),
        P(("enc", "dp"), None, None),
        P(None, "enc"),
        P(None, "enc"),
        P("dp", None),
        P("dp", None, "enc"),
    )
    out_specs = (
        P("dp", None, "enc"),
        P("dp", None, "enc"),
        P(("enc", "dp"), None, None),
        P("dp", "enc"),
        P("dp", "enc"),
    )
    return jax.shard_map(body, mesh=mesh, in_specs=in_specs, out_specs=out_specs, check_vma=False)
```

```python
import functools
import math

import jax
import jax.numpy as jnp
from jax import lax
from jax.experimental import pallas as pl
from jax.experimental.pallas import tpu as pltpu
from jax.sharding import PartitionSpec as P

D_HEAD = 128
EPSILON = 1e-06
BOTH = ("enc", "dp")
CHUNKS = (8, 8)
PER_STEP = 4
PIECES = 4
LANES = 128
EXTRA = 8
SPREAD_TILE = 16
PLACE_TILE = 512
FAR_FIRST = (2, 1, -1)
F32 = jnp.float32
BF16 = jnp.bfloat16
ROWS = (((0,), (0,)), ((), ()))
COLS = (((1,), (1,)), ((), ()))


def mm(a, b, dims=(((1,), (0,)), ((), ()))):
    return lax.dot_general(a, b, dims, preferred_element_type=F32)


def mean(value):
    return jnp.mean(value, axis=-1, keepdims=True)


def cuts(piece, rows, last):
    return [(0, rows // 2), (rows // 2, rows)] if last and piece else [(0, rows)]


def attention_kernel(first, last, *refs):
    x_refs, (q_ref, do_ref, w_ref) = refs[:PIECES], refs[PIECES : PIECES + 3]
    acc_in = None if first else refs[PIECES + 3]
    att_ref, dq_ref, *part_refs, dw_ref, acc = refs[PIECES + (3 if first else 6) :]
    step = pl.program_id(0)
    inverse = 1.0 / math.sqrt(D_HEAD)
    per_step, span, cols = q_ref.shape
    pairs, rows, width = x_refs[0].shape
    knb = pairs // per_step
    heads = cols // D_HEAD

    @pl.when(step == 0)
    def _():
        acc[...] = jnp.zeros_like(acc) if first else acc_in[...]

    heads_at = [slice(h * D_HEAD, (h + 1) * D_HEAD) for h in range(heads)]
    each = lambda f, *lists: [f(*parts) for parts in zip(*lists)]
    x = jnp.concatenate(
        [ref[s * knb : (s + 1) * knb].reshape(knb * rows, width) for s in range(per_step) for ref in x_refs], axis=0
    )
    count = knb * rows * len(x_refs)
    spans = [slice(s * count, (s + 1) * count) for s in range(per_step)]
    both = [(s, at) for s in range(per_step) for at in heads_at]
    queries = [q_ref[s, :, at].astype(F32) for s, at in both]
    grads = [do_ref[s, :, at] for s, at in both]
    query_scales = each(lambda q: lax.rsqrt(mean(q * q) + EPSILON), queries)
    query_units = each(lambda q, c: q * c, queries, query_scales)
    query_bfs = each(lambda u: u.astype(BF16), query_units)
    keys_all = mm(x, w_ref[:, :cols]).astype(BF16).astype(F32)
    keys = [keys_all[spans[s], at] for s, at in both]
    key_scales = each(lambda k: lax.rsqrt(mean(k * k) + EPSILON), keys)
    key_units = each(lambda k, c: k * c, keys, key_scales)
    key_bfs = each(lambda u: u.astype(BF16), key_units)
    values_all = mm(x, w_ref[:, cols:]).astype(BF16)
    values = [values_all[spans[s], at] for s, at in both]
    blank = jnp.zeros((span, D_HEAD), BF16)
    rows_of = lambda top, bottom: jnp.concatenate([top, bottom], axis=0)
    cols_of = lambda left, right: jnp.concatenate([left, right], axis=1)
    outer = each(lambda q, g: rows_of(cols_of(q, blank), cols_of(blank, g)), query_bfs, grads)
    inner = each(cols_of, key_bfs, values)
    products = each(lambda o, i: mm(o, i, COLS), outer, inner)
    raised = each(lambda p: jnp.exp(p[:span] * inverse), products)
    d_probs = each(lambda p: p[span:], products)
    weights = each(lambda e: e * (1.0 / jnp.sum(e, axis=-1, keepdims=True)), raised)
    probs = each(lambda p: p.astype(BF16), weights)
    d_scores = each(
        lambda p, d: (p * (d - jnp.sum(d * p, axis=-1, keepdims=True)) * inverse).astype(BF16), weights, d_probs
    )
    middle = each(rows_of, d_scores, probs)
    to_queries = each(mm, middle, inner)
    to_keys = each(lambda m, o: mm(m, o, ROWS), middle, outer)
    d_query_units = each(lambda t: t[:span, :D_HEAD], to_queries)
    attended = each(lambda t: t[span:, D_HEAD:].astype(BF16), to_queries)
    d_key_units = each(lambda t: t[:, :D_HEAD], to_keys)
    d_values = each(lambda t: t[:, D_HEAD:].astype(BF16), to_keys)
    d_queries = each(
        lambda c, d, u: (c * (d - u * mean(d * u))).astype(BF16), query_scales, d_query_units, query_units
    )
    d_keys = each(lambda c, d, u: (c * (d - u * mean(d * u))).astype(BF16), key_scales, d_key_units, key_units)
    d_kv = []
    for s in range(per_step):
        mine = slice(s * heads, (s + 1) * heads)
        att_ref[s] = jnp.concatenate(attended[mine], axis=1)
        dq_ref[s] = jnp.concatenate(d_queries[mine], axis=1)
        d_kv.append(jnp.concatenate(d_keys[mine] + d_values[mine], axis=1))
    d_kv = jnp.concatenate(d_kv, axis=0)
    part = mm(d_kv, w_ref[...], COLS).astype(BF16)
    for s in range(per_step):
        outs = iter(part_refs)
        for i in range(PIECES):
            at = s * count + i * knb * rows
            piece = part[at : at + knb * rows].reshape(knb, rows, width)
            for low, high in cuts(i, rows, last):
                next(outs)[s * knb : (s + 1) * knb] = piece[:, low:high]
    acc[...] += mm(x, d_kv, ROWS)

    @pl.when(step == pl.num_programs(0) - 1)
    def _():
        dw_ref[...] = acc[...].astype(dw_ref.dtype)


def attention(chunk, pieces, queries, d_out, w, carried):
    _, span, cols = queries.shape
    pairs, rows, width = pieces[0].shape
    mine = CHUNKS[chunk]
    knb = pairs // mine
    steps = mine // PER_STEP
    first, last = chunk == 0, chunk == len(CHUNKS) - 1
    offset = sum(CHUNKS[:chunk]) // PER_STEP
    by_stretch = pl.BlockSpec((PER_STEP, span, cols), lambda i: (offset + i, 0, 0))
    by_pair = pl.BlockSpec((PER_STEP * knb, rows, width), lambda i: (i, 0, 0))
    whole = pl.BlockSpec(w.shape, lambda i: (0, 0))
    in_specs = [by_pair] * PIECES + [by_stretch] * 2 + [whole]
    args = [*pieces, queries, d_out, w]
    aliases = {}
    if not first:
        att, dq, acc = carried
        in_specs += [whole, pl.BlockSpec(memory_space=pl.ANY), pl.BlockSpec(memory_space=pl.ANY)]
        args += [acc, att, dq]
        aliases = {PIECES + 4: 0, PIECES + 5: 1}
    sizes = [high - low for i in range(PIECES) for low, high in cuts(i, rows, last)]
    out = pl.pallas_call(
        functools.partial(attention_kernel, first, last),
        grid=(steps,),
        in_specs=in_specs,
        out_specs=[by_stretch, by_stretch]
        + [pl.BlockSpec((PER_STEP * knb, size, width), lambda i: (i, 0, 0)) for size in sizes]
        + [whole],
        out_shape=[jax.ShapeDtypeStruct(queries.shape, BF16)] * 2
        + [jax.ShapeDtypeStruct((pairs, size, width), BF16) for size in sizes]
        + [jax.ShapeDtypeStruct(w.shape, BF16 if last else F32)],
        scratch_shapes=[pltpu.VMEM(w.shape, F32)],
        input_output_aliases=aliases,
        compiler_params=pltpu.CompilerParams(vmem_limit_bytes=40 * 1024 * 1024),
        cost_estimate=pl.CostEstimate(
            flops=mine * 900_000_000, bytes_accessed=mine * 800_000, transcendentals=mine * 66_000
        ),
        name="attention",
    )(*args)
    return out[2:-1], (out[0], out[1], out[-1])


def spread_kernel(x_ref, ids_ref, out_ref):
    held, rows, width = x_ref.shape
    count = held * SPREAD_TILE
    at = lax.broadcasted_iota(jnp.int32, (count, count), 0)
    source = lax.rem(at, held) * SPREAD_TILE + at // held
    turn = (source == lax.broadcasted_iota(jnp.int32, (count, count), 1)).astype(BF16)
    blocks = width // LANES
    out_ref[:, blocks * held :] = jnp.broadcast_to(ids_ref[...], (rows, EXTRA, LANES))
    for r in range(0, rows, SPREAD_TILE):
        turned = mm(turn, x_ref[:, r : r + SPREAD_TILE].reshape(count, width)).astype(BF16)
        turned = turned.reshape(SPREAD_TILE, held, width)
        for i in range(blocks):
            out_ref[r : r + SPREAD_TILE, i * held : (i + 1) * held] = turned[:, :, i * LANES : (i + 1) * LANES]


def spread_rows(x, ids):
    held, rows, width = x.shape
    lines = width // LANES * held + EXTRA
    return pl.pallas_call(
        spread_kernel,
        in_specs=[pl.BlockSpec(memory_space=pltpu.VMEM)] * 2,
        out_specs=pl.BlockSpec(memory_space=pltpu.VMEM),
        out_shape=jax.ShapeDtypeStruct((rows, lines, LANES), BF16),
        compiler_params=pltpu.CompilerParams(vmem_limit_bytes=32 * 1024 * 1024),
        name="spread_rows",
    )(x, ids)


def gather_kernel(x_ref, out_ref):
    rows, held, width = x_ref.shape
    count = held * SPREAD_TILE
    at = lax.broadcasted_iota(jnp.int32, (count, count), 0)
    source = lax.rem(at, SPREAD_TILE) * held + at // SPREAD_TILE
    turn = (source == lax.broadcasted_iota(jnp.int32, (count, count), 1)).astype(BF16)
    for r in range(0, rows, SPREAD_TILE):
        turned = mm(turn, x_ref[r : r + SPREAD_TILE].reshape(count, width)).astype(BF16)
        out_ref[:, r : r + SPREAD_TILE] = turned.reshape(held, SPREAD_TILE, width)


def gather_rows(x):
    rows, held, width = x.shape
    return pl.pallas_call(
        gather_kernel,
        in_specs=[pl.BlockSpec(memory_space=pltpu.VMEM)],
        out_specs=pl.BlockSpec(memory_space=pltpu.VMEM),
        out_shape=jax.ShapeDtypeStruct((held, rows, width), BF16),
        compiler_params=pltpu.CompilerParams(vmem_limit_bytes=32 * 1024 * 1024),
        name="gather_rows",
    )(x)


def pick_first_kernel(held, shards, first, table_ref, out_ref):
    senders, lines, lanes = table_ref.shape
    count, wanted = senders * held, out_ref.shape[0]
    each = wanted // shards
    ends = table_ref[:shards, lines - EXTRA :].astype(F32)
    row = lax.broadcasted_iota(jnp.int32, (wanted, shards), 0)
    owner = (row // each == lax.broadcasted_iota(jnp.int32, (wanted, shards), 1)).astype(BF16)
    high, low = (mm(owner, ends[:, i].astype(BF16)) for i in range(2))
    lane = lax.broadcasted_iota(jnp.int32, (wanted, lanes), 1)
    mine = lane == lax.rem(lax.broadcasted_iota(jnp.int32, (wanted, lanes), 0), each) + first
    ids = jnp.sum(jnp.where(mine, high * held + low, 0.0), axis=-1, keepdims=True).astype(jnp.int32)
    hit = (ids == lax.broadcasted_iota(jnp.int32, (wanted, count), 1)).astype(BF16)
    blocks = [table_ref[:, at : at + held].reshape(count, lanes) for at in range(0, lines - EXTRA, held)]
    for i in range(0, len(blocks), 2):
        picked = mm(hit, jnp.concatenate(blocks[i : i + 2], axis=1))
        out_ref[:, i * lanes : (i + 2) * lanes] = picked.astype(BF16)


def pick_first_rows(table, held, shards, first, each):
    senders, lines, lanes = table.shape
    width = (lines - EXTRA) // held * lanes
    return pl.pallas_call(
        functools.partial(pick_first_kernel, held, shards, first),
        in_specs=[pl.BlockSpec(memory_space=pltpu.VMEM)],
        out_specs=pl.BlockSpec(memory_space=pltpu.VMEM),
        out_shape=jax.ShapeDtypeStruct((shards * each, width), BF16),
        compiler_params=pltpu.CompilerParams(vmem_limit_bytes=32 * 1024 * 1024),
        name="pick_first_rows",
    )(table)


def pick_kernel(held, ids_ref, table_ref, out_ref):
    ids = ids_ref[...]
    senders, lines, lanes = table_ref.shape
    count = senders * held
    hit = (ids == lax.broadcasted_iota(jnp.int32, (ids.shape[0], count), 1)).astype(BF16)
    blocks = [table_ref[:, at : at + held].reshape(count, lanes) for at in range(0, lines - EXTRA, held)]
    for i in range(0, len(blocks), 2):
        picked = mm(hit, jnp.concatenate(blocks[i : i + 2], axis=1))
        out_ref[:, i * lanes : (i + 2) * lanes] = picked.astype(BF16)


def pick_rows(ids, table, held):
    senders, lines, lanes = table.shape
    width = (lines - EXTRA) // held * lanes
    return pl.pallas_call(
        functools.partial(pick_kernel, held),
        in_specs=[pl.BlockSpec(memory_space=pltpu.VMEM)] * 2,
        out_specs=pl.BlockSpec(memory_space=pltpu.VMEM),
        out_shape=jax.ShapeDtypeStruct((ids.shape[0], width), BF16),
        compiler_params=pltpu.CompilerParams(vmem_limit_bytes=32 * 1024 * 1024),
        name="pick_rows",
    )(ids.reshape(-1, 1), table)


def place_kernel(ids_ref, rows_ref, out_ref):
    ids = ids_ref[...]
    for at in range(0, out_ref.shape[0], PLACE_TILE):
        row = lax.broadcasted_iota(jnp.int32, (PLACE_TILE, ids.shape[1]), 0) + at
        out_ref[at : at + PLACE_TILE] = mm((ids == row).astype(BF16), rows_ref[...]).astype(BF16)


def place_rows(ids, rows, count):
    return pl.pallas_call(
        place_kernel,
        in_specs=[pl.BlockSpec(memory_space=pltpu.VMEM)] * 2,
        out_specs=pl.BlockSpec(memory_space=pltpu.VMEM),
        out_shape=jax.ShapeDtypeStruct((count, rows.shape[1]), BF16),
        compiler_params=pltpu.CompilerParams(vmem_limit_bytes=32 * 1024 * 1024),
        name="place_rows",
    )(ids.reshape(1, -1), rows)


def shift(value, by):
    count = lax.axis_size("enc")
    return lax.ppermute(value, "enc", [(i, (i + by) % count) for i in range(count)])


def gather_pieces(own):
    return [own] + [shift(own, by) for by in FAR_FIRST]


def sum_pieces(parts):
    back = [shift(part, -by) for by, part in zip(FAR_FIRST, parts[1:])]
    return sum(part.astype(F32) for part in [parts[0], *back]).astype(BF16)


def sum_halves(parts, earlier):
    own, far_a, far_b, left_a, left_b, right_a, right_b = parts
    add = lambda *terms: sum(term.astype(F32) for term in terms).astype(BF16)
    far_a, far_b = shift(far_a, 1), shift(far_b, -1)
    right_b, left_a = shift(right_b, 1), shift(left_a, -1)
    far_a, far_b, *earlier = lax.optimization_barrier((far_a, far_b, *earlier))
    right_a, left_b = shift(add(right_a, far_a), 1), shift(add(left_b, far_b), -1)
    return *earlier, add(own, jnp.concatenate([right_a, right_b], axis=1), jnp.concatenate([left_a, left_b], axis=1))


def body(queries, encodings, w_key, w_value, neighbours, d_out):
    enc_count = lax.axis_size("enc")
    shards = lax.axis_size("dp")
    devices = enc_count * shards
    held, neigh_len, width = encodings.shape
    stretches, _, cols = queries.shape
    pair_count = neighbours.size
    w = jnp.concatenate([w_key, w_value], axis=1)
    blocks = width // LANES
    own_ids = neighbours.reshape(-1)
    own_ids = jnp.stack([own_ids // held, own_ids % held]).astype(BF16)
    by_row = spread_rows(encodings, jnp.pad(own_ids, ((0, EXTRA - 2), (0, LANES - pair_count))))
    table = lax.all_to_all(by_row, BOTH, 0, 0, tiled=True)
    ids = table[:shards, blocks * held : blocks * held + 2, :pair_count].astype(jnp.int32)
    ids = ids[:, 0] * held + ids[:, 1]
    knb = pair_count // stretches
    sent, start = [], 0
    for size in CHUNKS:
        if start == 0:
            sent.append(pick_first_rows(table, held, shards, 0, size * knb))
        else:
            wanted = ids[:, start * knb : (start + size) * knb]
            sent.append(pick_rows(wanted.reshape(-1), table, held))
        sent[-1] = sent[-1].reshape(shards, size * knb, width)
        start += size
    pieces = []
    for c in range(len(CHUNKS)):
        if c > 0:
            sent[c], own = lax.optimization_barrier((sent[c], own))
            pieces.append(gather_pieces(own))
        own = jnp.swapaxes(lax.all_to_all(sent[c], "dp", 0, 0, tiled=True), 0, 1)
    pieces.append(gather_pieces(own))
    carried = None
    returned = []
    for c in range(len(CHUNKS)):
        parts, carried = attention(c, pieces[c], queries, d_out, w, carried)
        if c < len(CHUNKS) - 1:
            returned.append(sum_pieces(parts))
    returned = sum_halves(parts, returned)
    att, dq, acc = carried
    d_w = lax.all_to_all(acc.reshape(shards, -1, 2 * cols), "dp", 0, 0, tiled=True)
    summed = jnp.swapaxes(jnp.concatenate(returned, axis=0), 0, 1)
    summed, d_w = lax.optimization_barrier((summed, d_w))
    rows = lax.all_to_all(summed, "dp", 0, 0, tiled=True).reshape(shards * pair_count, width)
    placed = place_rows(ids.reshape(-1), rows, devices * held).reshape(devices, held, width)
    d_encodings = gather_rows(lax.all_to_all(placed, BOTH, 0, 0, tiled=True))
    d_w = jnp.sum(d_w.astype(F32), axis=0)
    return att, dq, d_encodings, d_w[:, :cols], d_w[:, cols:]


def solution(mesh):
    in_specs = (
        P("dp", None, "enc"),
        P(("enc", "dp"), None, None),
        P(None, "enc"),
        P(None, "enc"),
        P("dp", None),
        P("dp", None, "enc"),
    )
    out_specs = (
        P("dp", None, "enc"),
        P("dp", None, "enc"),
        P(("enc", "dp"), None, None),
        P("dp", "enc"),
        P("dp", "enc"),
    )
    return jax.shard_map(body, mesh=mesh, in_specs=in_specs, out_specs=out_specs, check_vma=False)
```

```python
import functools
import math

import jax
import jax.numpy as jnp
from jax import lax
from jax.experimental import pallas as pl
from jax.experimental.pallas import tpu as pltpu
from jax.sharding import PartitionSpec as P

D_HEAD = 128
EPSILON = 1e-06
BOTH = ("enc", "dp")
CHUNKS = (8, 8)
PER_STEP = 4
PIECES = 4
LANES = 128
EXTRA = 8
SPREAD_TILE = 16
PLACE_TILE = 512
FAR_FIRST = (2, 1, -1)
F32 = jnp.float32
BF16 = jnp.bfloat16
ROWS = (((0,), (0,)), ((), ()))
COLS = (((1,), (1,)), ((), ()))


def mm(a, b, dims=(((1,), (0,)), ((), ()))):
    return lax.dot_general(a, b, dims, preferred_element_type=F32)


def mean(value):
    return jnp.mean(value, axis=-1, keepdims=True)


def cuts(piece, rows, last):
    return [(0, rows // 2), (rows // 2, rows)] if last and piece else [(0, rows)]


def attention_kernel(first, last, *refs):
    x_refs, (q_ref, do_ref, w_ref) = refs[:PIECES], refs[PIECES : PIECES + 3]
    acc_in = None if first else refs[PIECES + 3]
    att_ref, dq_ref, *part_refs, dw_ref, acc = refs[PIECES + (3 if first else 6) :]
    step = pl.program_id(0)
    inverse = 1.0 / math.sqrt(D_HEAD)
    per_step, span, cols = q_ref.shape
    pairs, rows, width = x_refs[0].shape
    knb = pairs // per_step
    heads = cols // D_HEAD

    @pl.when(step == 0)
    def _():
        acc[...] = jnp.zeros_like(acc) if first else acc_in[...]

    heads_at = [slice(h * D_HEAD, (h + 1) * D_HEAD) for h in range(heads)]
    each = lambda f, *lists: [f(*parts) for parts in zip(*lists)]
    x = jnp.concatenate(
        [ref[s * knb : (s + 1) * knb].reshape(knb * rows, width) for s in range(per_step) for ref in x_refs], axis=0
    )
    count = knb * rows * len(x_refs)
    spans = [slice(s * count, (s + 1) * count) for s in range(per_step)]
    both = [(s, at) for s in range(per_step) for at in heads_at]
    queries = [q_ref[s, :, at].astype(F32) for s, at in both]
    grads = [do_ref[s, :, at] for s, at in both]
    query_scales = each(lambda q: lax.rsqrt(mean(q * q) + EPSILON), queries)
    query_units = each(lambda q, c: q * c, queries, query_scales)
    query_bfs = each(lambda u: u.astype(BF16), query_units)
    keys_all = mm(x, w_ref[:, :cols]).astype(BF16).astype(F32)
    keys = [keys_all[spans[s], at] for s, at in both]
    key_scales = each(lambda k: lax.rsqrt(mean(k * k) + EPSILON), keys)
    key_units = each(lambda k, c: k * c, keys, key_scales)
    key_bfs = each(lambda u: u.astype(BF16), key_units)
    values_all = mm(x, w_ref[:, cols:]).astype(BF16)
    values = [values_all[spans[s], at] for s, at in both]
    blank = jnp.zeros((span, D_HEAD), BF16)
    rows_of = lambda top, bottom: jnp.concatenate([top, bottom], axis=0)
    cols_of = lambda left, right: jnp.concatenate([left, right], axis=1)
    outer = each(lambda q, g: rows_of(cols_of(q, blank), cols_of(blank, g)), query_bfs, grads)
    inner = each(cols_of, key_bfs, values)
    products = each(lambda o, i: mm(o, i, COLS), outer, inner)
    raised = each(lambda p: jnp.exp(p[:span] * inverse), products)
    d_probs = each(lambda p: p[span:], products)
    weights = each(lambda e: e * (1.0 / jnp.sum(e, axis=-1, keepdims=True)), raised)
    probs = each(lambda p: p.astype(BF16), weights)
    d_scores = each(
        lambda p, d: (p * (d - jnp.sum(d * p, axis=-1, keepdims=True)) * inverse).astype(BF16), weights, d_probs
    )
    middle = each(rows_of, d_scores, probs)
    to_queries = each(mm, middle, inner)
    to_keys = each(lambda m, o: mm(m, o, ROWS), middle, outer)
    d_query_units = each(lambda t: t[:span, :D_HEAD], to_queries)
    attended = each(lambda t: t[span:, D_HEAD:].astype(BF16), to_queries)
    d_key_units = each(lambda t: t[:, :D_HEAD], to_keys)
    d_values = each(lambda t: t[:, D_HEAD:].astype(BF16), to_keys)
    d_queries = each(
        lambda c, d, u: (c * (d - u * mean(d * u))).astype(BF16), query_scales, d_query_units, query_units
    )
    d_keys = each(lambda c, d, u: (c * (d - u * mean(d * u))).astype(BF16), key_scales, d_key_units, key_units)
    d_kv = []
    for s in range(per_step):
        mine = slice(s * heads, (s + 1) * heads)
        att_ref[s] = jnp.concatenate(attended[mine], axis=1)
        dq_ref[s] = jnp.concatenate(d_queries[mine], axis=1)
        d_kv.append(jnp.concatenate(d_keys[mine] + d_values[mine], axis=1))
    d_kv = jnp.concatenate(d_kv, axis=0)
    part = mm(d_kv, w_ref[...], COLS).astype(BF16)
    for s in range(per_step):
        outs = iter(part_refs)
        for i in range(PIECES):
            at = s * count + i * knb * rows
            piece = part[at : at + knb * rows].reshape(knb, rows, width)
            for low, high in cuts(i, rows, last):
                next(outs)[s * knb : (s + 1) * knb] = piece[:, low:high]
    acc[...] += mm(x, d_kv, ROWS)

    @pl.when(step == pl.num_programs(0) - 1)
    def _():
        dw_ref[...] = acc[...].astype(dw_ref.dtype)


def attention(chunk, pieces, queries, d_out, w, carried):
    _, span, cols = queries.shape
    pairs, rows, width = pieces[0].shape
    mine = CHUNKS[chunk]
    knb = pairs // mine
    steps = mine // PER_STEP
    first, last = chunk == 0, chunk == len(CHUNKS) - 1
    offset = sum(CHUNKS[:chunk]) // PER_STEP
    by_stretch = pl.BlockSpec((PER_STEP, span, cols), lambda i: (offset + i, 0, 0))
    by_pair = pl.BlockSpec((PER_STEP * knb, rows, width), lambda i: (i, 0, 0))
    whole = pl.BlockSpec(w.shape, lambda i: (0, 0))
    in_specs = [by_pair] * PIECES + [by_stretch] * 2 + [whole]
    args = [*pieces, queries, d_out, w]
    aliases = {}
    if not first:
        att, dq, acc = carried
        in_specs += [whole, pl.BlockSpec(memory_space=pl.ANY), pl.BlockSpec(memory_space=pl.ANY)]
        args += [acc, att, dq]
        aliases = {PIECES + 4: 0, PIECES + 5: 1}
    sizes = [high - low for i in range(PIECES) for low, high in cuts(i, rows, last)]
    out = pl.pallas_call(
        functools.partial(attention_kernel, first, last),
        grid=(steps,),
        in_specs=in_specs,
        out_specs=[by_stretch, by_stretch]
        + [pl.BlockSpec((PER_STEP * knb, size, width), lambda i: (i, 0, 0)) for size in sizes]
        + [whole],
        out_shape=[jax.ShapeDtypeStruct(queries.shape, BF16)] * 2
        + [jax.ShapeDtypeStruct((pairs, size, width), BF16) for size in sizes]
        + [jax.ShapeDtypeStruct(w.shape, BF16 if last else F32)],
        scratch_shapes=[pltpu.VMEM(w.shape, F32)],
        input_output_aliases=aliases,
        compiler_params=pltpu.CompilerParams(vmem_limit_bytes=40 * 1024 * 1024),
        cost_estimate=pl.CostEstimate(
            flops=mine * 900_000_000, bytes_accessed=mine * 800_000, transcendentals=mine * 66_000
        ),
        name="attention",
    )(*args)
    return out[2:-1], (out[0], out[1], out[-1])


def spread_kernel(x_ref, ids_ref, out_ref):
    held, rows, width = x_ref.shape
    count = held * SPREAD_TILE
    at = lax.broadcasted_iota(jnp.int32, (count, count), 0)
    source = lax.rem(at, held) * SPREAD_TILE + at // held
    turn = (source == lax.broadcasted_iota(jnp.int32, (count, count), 1)).astype(BF16)
    blocks = width // LANES
    out_ref[:, blocks * held :] = jnp.broadcast_to(ids_ref[...], (rows, EXTRA, LANES))
    for r in range(0, rows, SPREAD_TILE):
        turned = mm(turn, x_ref[:, r : r + SPREAD_TILE].reshape(count, width)).astype(BF16)
        turned = turned.reshape(SPREAD_TILE, held, width)
        for i in range(blocks):
            out_ref[r : r + SPREAD_TILE, i * held : (i + 1) * held] = turned[:, :, i * LANES : (i + 1) * LANES]


def spread_rows(x, ids):
    held, rows, width = x.shape
    lines = width // LANES * held + EXTRA
    return pl.pallas_call(
        spread_kernel,
        in_specs=[pl.BlockSpec(memory_space=pltpu.VMEM)] * 2,
        out_specs=pl.BlockSpec(memory_space=pltpu.VMEM),
        out_shape=jax.ShapeDtypeStruct((rows, lines, LANES), BF16),
        compiler_params=pltpu.CompilerParams(vmem_limit_bytes=32 * 1024 * 1024),
        name="spread_rows",
    )(x, ids)


def gather_kernel(x_ref, out_ref):
    rows, held, width = x_ref.shape
    count = held * SPREAD_TILE
    at = lax.broadcasted_iota(jnp.int32, (count, count), 0)
    source = lax.rem(at, SPREAD_TILE) * held + at // SPREAD_TILE
    turn = (source == lax.broadcasted_iota(jnp.int32, (count, count), 1)).astype(BF16)
    for r in range(0, rows, SPREAD_TILE):
        turned = mm(turn, x_ref[r : r + SPREAD_TILE].reshape(count, width)).astype(BF16)
        out_ref[:, r : r + SPREAD_TILE] = turned.reshape(held, SPREAD_TILE, width)


def gather_rows(x):
    rows, held, width = x.shape
    return pl.pallas_call(
        gather_kernel,
        in_specs=[pl.BlockSpec(memory_space=pltpu.VMEM)],
        out_specs=pl.BlockSpec(memory_space=pltpu.VMEM),
        out_shape=jax.ShapeDtypeStruct((held, rows, width), BF16),
        compiler_params=pltpu.CompilerParams(vmem_limit_bytes=32 * 1024 * 1024),
        name="gather_rows",
    )(x)


def pick_first_kernel(held, shards, first, table_ref, out_ref):
    senders, lines, lanes = table_ref.shape
    count, wanted = senders * held, out_ref.shape[0]
    each = wanted // shards
    ends = table_ref[:shards, lines - EXTRA :].astype(F32)
    row = lax.broadcasted_iota(jnp.int32, (wanted, shards), 0)
    owner = (row // each == lax.broadcasted_iota(jnp.int32, (wanted, shards), 1)).astype(BF16)
    high, low = (mm(owner, ends[:, i].astype(BF16)) for i in range(2))
    lane = lax.broadcasted_iota(jnp.int32, (wanted, lanes), 1)
    mine = lane == lax.rem(lax.broadcasted_iota(jnp.int32, (wanted, lanes), 0), each) + first
    ids = jnp.sum(jnp.where(mine, high * held + low, 0.0), axis=-1, keepdims=True).astype(jnp.int32)
    hit = (ids == lax.broadcasted_iota(jnp.int32, (wanted, count), 1)).astype(BF16)
    blocks = [table_ref[:, at : at + held].reshape(count, lanes) for at in range(0, lines - EXTRA, held)]
    for i in range(0, len(blocks), 2):
        picked = mm(hit, jnp.concatenate(blocks[i : i + 2], axis=1))
        out_ref[:, i * lanes : (i + 2) * lanes] = picked.astype(BF16)


def pick_first_rows(table, held, shards, first, each):
    senders, lines, lanes = table.shape
    width = (lines - EXTRA) // held * lanes
    return pl.pallas_call(
        functools.partial(pick_first_kernel, held, shards, first),
        in_specs=[pl.BlockSpec(memory_space=pltpu.VMEM)],
        out_specs=pl.BlockSpec(memory_space=pltpu.VMEM),
        out_shape=jax.ShapeDtypeStruct((shards * each, width), BF16),
        compiler_params=pltpu.CompilerParams(vmem_limit_bytes=32 * 1024 * 1024),
        name="pick_first_rows",
    )(table)


def pick_kernel(held, ids_ref, table_ref, out_ref):
    ids = ids_ref[...]
    senders, lines, lanes = table_ref.shape
    count = senders * held
    hit = (ids == lax.broadcasted_iota(jnp.int32, (ids.shape[0], count), 1)).astype(BF16)
    blocks = [table_ref[:, at : at + held].reshape(count, lanes) for at in range(0, lines - EXTRA, held)]
    for i in range(0, len(blocks), 2):
        picked = mm(hit, jnp.concatenate(blocks[i : i + 2], axis=1))
        out_ref[:, i * lanes : (i + 2) * lanes] = picked.astype(BF16)


def pick_rows(ids, table, held):
    senders, lines, lanes = table.shape
    width = (lines - EXTRA) // held * lanes
    return pl.pallas_call(
        functools.partial(pick_kernel, held),
        in_specs=[pl.BlockSpec(memory_space=pltpu.VMEM)] * 2,
        out_specs=pl.BlockSpec(memory_space=pltpu.VMEM),
        out_shape=jax.ShapeDtypeStruct((ids.shape[0], width), BF16),
        compiler_params=pltpu.CompilerParams(vmem_limit_bytes=32 * 1024 * 1024),
        name="pick_rows",
    )(ids.reshape(-1, 1), table)


def place_kernel(ids_ref, rows_ref, out_ref):
    ids = ids_ref[...]
    for at in range(0, out_ref.shape[0], PLACE_TILE):
        row = lax.broadcasted_iota(jnp.int32, (PLACE_TILE, ids.shape[1]), 0) + at
        out_ref[at : at + PLACE_TILE] = mm((ids == row).astype(BF16), rows_ref[...]).astype(BF16)


def place_rows(ids, rows, count):
    return pl.pallas_call(
        place_kernel,
        in_specs=[pl.BlockSpec(memory_space=pltpu.VMEM)] * 2,
        out_specs=pl.BlockSpec(memory_space=pltpu.VMEM),
        out_shape=jax.ShapeDtypeStruct((count, rows.shape[1]), BF16),
        compiler_params=pltpu.CompilerParams(vmem_limit_bytes=60 * 1024 * 1024),
        name="place_rows",
    )(ids.reshape(1, -1), rows)


def shift(value, by):
    count = lax.axis_size("enc")
    return lax.ppermute(value, "enc", [(i, (i + by) % count) for i in range(count)])


def gather_pieces(own):
    return [own] + [shift(own, by) for by in FAR_FIRST]


def sum_pieces(parts):
    back = [shift(part, -by) for by, part in zip(FAR_FIRST, parts[1:])]
    return sum(part.astype(F32) for part in [parts[0], *back]).astype(BF16)


def sum_halves(parts, earlier):
    own, far_a, far_b, left_a, left_b, right_a, right_b = parts
    add = lambda *terms: sum(term.astype(F32) for term in terms).astype(BF16)
    far_a, far_b = shift(far_a, 1), shift(far_b, -1)
    right_b, left_a = shift(right_b, 1), shift(left_a, -1)
    far_a, far_b, *earlier = lax.optimization_barrier((far_a, far_b, *earlier))
    right_a, left_b = shift(add(right_a, far_a), 1), shift(add(left_b, far_b), -1)
    return *earlier, add(own, jnp.concatenate([right_a, right_b], axis=1), jnp.concatenate([left_a, left_b], axis=1))


def body(queries, encodings, w_key, w_value, neighbours, d_out):
    enc_count = lax.axis_size("enc")
    shards = lax.axis_size("dp")
    devices = enc_count * shards
    held, neigh_len, width = encodings.shape
    stretches, _, cols = queries.shape
    pair_count = neighbours.size
    w = jnp.concatenate([w_key, w_value], axis=1)
    blocks = width // LANES
    own_ids = neighbours.reshape(-1)
    own_ids = jnp.stack([own_ids // held, own_ids % held]).astype(BF16)
    by_row = spread_rows(encodings, jnp.pad(own_ids, ((0, EXTRA - 2), (0, LANES - pair_count))))
    table = lax.all_to_all(by_row, BOTH, 0, 0, tiled=True)
    ids = table[:shards, blocks * held : blocks * held + 2, :pair_count].astype(jnp.int32)
    ids = ids[:, 0] * held + ids[:, 1]
    knb = pair_count // stretches
    sent, start = [], 0
    for size in CHUNKS:
        if start == 0:
            sent.append(pick_first_rows(table, held, shards, 0, size * knb))
        else:
            wanted = ids[:, start * knb : (start + size) * knb]
            sent.append(pick_rows(wanted.reshape(-1), table, held))
        sent[-1] = sent[-1].reshape(shards, size * knb, width)
        start += size
    pieces = []
    for c in range(len(CHUNKS)):
        if c > 0:
            sent[c], own = lax.optimization_barrier((sent[c], own))
            pieces.append(gather_pieces(own))
        own = jnp.swapaxes(lax.all_to_all(sent[c], "dp", 0, 0, tiled=True), 0, 1)
    pieces.append(gather_pieces(own))
    carried = None
    returned = []
    for c in range(len(CHUNKS)):
        parts, carried = attention(c, pieces[c], queries, d_out, w, carried)
        if c < len(CHUNKS) - 1:
            returned.append(sum_pieces(parts))
    returned = sum_halves(parts, returned)
    att, dq, acc = carried
    d_w = lax.all_to_all(acc.reshape(shards, -1, 2 * cols), "dp", 0, 0, tiled=True)
    summed = jnp.swapaxes(jnp.concatenate(returned, axis=0), 0, 1)
    summed, d_w = lax.optimization_barrier((summed, d_w))
    rows = lax.all_to_all(summed, "dp", 0, 0, tiled=True).reshape(shards * pair_count, width)
    placed = place_rows(ids.reshape(-1), rows, devices * held).reshape(devices, held, width)
    d_encodings = gather_rows(lax.all_to_all(placed, BOTH, 0, 0, tiled=True))
    d_w = jnp.sum(d_w.astype(F32), axis=0)
    return att, dq, d_encodings, d_w[:, :cols], d_w[:, cols:]


def solution(mesh):
    in_specs = (
        P("dp", None, "enc"),
        P(("enc", "dp"), None, None),
        P(None, "enc"),
        P(None, "enc"),
        P("dp", None),
        P("dp", None, "enc"),
    )
    out_specs = (
        P("dp", None, "enc"),
        P("dp", None, "enc"),
        P(("enc", "dp"), None, None),
        P("dp", "enc"),
        P("dp", "enc"),
    )
    return jax.shard_map(body, mesh=mesh, in_specs=in_specs, out_specs=out_specs, check_vma=False)
```
